32 devices in a mesh: fsdp: 32 (over z, y, x, core).
Axes of the slice: x: 2, y: 2, z: 4, core: 2. Of those that a mesh axis runs over, the one named last changes fastest.
Arguments:
- tokens: bfloat16 [32768, 768], P('fsdp'), may hold values from -6 to 6
- encoder_states: bfloat16 [32768, 768], P('fsdp'), may hold values from -6 to 6
- self_query: bfloat16 [589824], P('fsdp'), may hold values from -0.109375 to 0.109375
- self_key: bfloat16 [589824], P('fsdp'), may hold values from -0.109375 to 0.109375
- self_value: bfloat16 [589824], P('fsdp'), may hold values from -0.21875 to 0.21875
- self_out: bfloat16 [589824], P('fsdp'), may hold values from -0.875 to 0.875
- cross_query: bfloat16 [589824], P('fsdp'), may hold values from -0.109375 to 0.109375
- cross_key: bfloat16 [589824], P('fsdp'), may hold values from -0.109375 to 0.109375
- cross_value: bfloat16 [589824], P('fsdp'), may hold values from -0.21875 to 0.21875
- cross_out: bfloat16 [589824], P('fsdp'), may hold values from -0.875 to 0.875
- ff_gate: bfloat16 [1572864], P('fsdp'), may hold values from -0.21875 to 0.21875
- ff_up: bfloat16 [1572864], P('fsdp'), may hold values from -0.21875 to 0.21875
- ff_down: bfloat16 [1572864], P('fsdp'), may hold values from -0.25 to 0.25
- norm_gains: bfloat16 [3, 768], replicated, may hold values from 0.5 to 1.5
- bias_table: bfloat16 [32, 12], replicated, may hold values from -4 to 4
- buckets: int32 [512, 512], replicated, may hold values from 0 to 31, as said below
- cotangent: bfloat16 [32768, 768], P('fsdp'), may hold values from -6 to 6
Outputs:
- output: bfloat16 [32768, 768], P('fsdp')
- tokens_grad: bfloat16 [32768, 768], P('fsdp')
- encoder_grad: bfloat16 [32768, 768], P('fsdp')
- grad_self_query: float32 [589824], P('fsdp')
- grad_self_key: float32 [589824], P('fsdp')
- grad_self_value: float32 [589824], P('fsdp')
- grad_self_out: float32 [589824], P('fsdp')
- grad_cross_query: float32 [589824], P('fsdp')
- grad_cross_key: float32 [589824], P('fsdp')
- grad_cross_value: float32 [589824], P('fsdp')
- grad_cross_out: float32 [589824], P('fsdp')
- grad_ff_gate: float32 [1572864], P('fsdp')
- grad_ff_up: float32 [1572864], P('fsdp')
- grad_ff_down: float32 [1572864], P('fsdp')
- gains_grad: float32 [3, 768], replicated
- table_grad: float32 [32, 12], replicated
The draws below stay inside these ranges and needn't reach their ends.
Inputs may be any that keep to these rules, and one draw needn't show every extreme that they name: buckets[i, j] depends only on i - j; it is 0 where j > i, equals i - j where i - j < 16, does not fall as i - j grows and is 31 at the largest distances.
All inputs are finite; a program needn't handle non-finite values.
Results may differ from the reference program's by a relative error of at most 0.025.
The reference program's roundings to bfloat16 on the way count: a program that leaves them out, or rounds other values in their place, can miss the bound.
Values may be sent and summed in bfloat16 or wider, within the bound.
No kernel may reach another device: no remote copies, remote signals or barrier semaphores. Data moves between devices by JAX's collectives and lax.ppermute only.
A program may use at most 256 MiB of HBM per device.

```python
import jax
import jax.numpy as jnp
from jax import lax

D = 768
HEADS = 12
HD = 64
FF = 2048
BUCKETS = 32
LEN = 512
ENC = 512
MICRO = 2
SEQ_MB = 1
INNER = 768
TOKENS = 32768
ENC_TOKENS = 32768


def draw_buckets(key, part):
    key = jax.random.fold_in(key, 11)
    spread = min(111, LEN - 18)
    chosen = jnp.sort(jax.random.permutation(key, spread)[:14]).astype(jnp.int32) + 17
    cut_points = jnp.concatenate([jnp.arange(1, 17, dtype=jnp.int32), chosen, jnp.full((1,), spread + 17, jnp.int32)])
    row_ids = lax.broadcasted_iota(jnp.int32, (LEN, LEN), 0)
    col_ids = lax.broadcasted_iota(jnp.int32, (LEN, LEN), 1)
    distance = row_ids - col_ids
    counted = jnp.sum((distance[:, :, None] >= cut_points[None, None, :]).astype(jnp.int32), axis=-1)
    return jnp.where(distance >= 0, counted, 0).astype(jnp.int32)


def strengthened(drawn, own_key, source, target, shards_of, factor):
    owner, partner = [(jnp.arange(drawn.shape[axis_at]) // (drawn.shape[axis_at] // shards_of)).reshape([-1 if axis == axis_at else 1 for axis in range(drawn.ndim)]) for axis_at in (source, target)]
    chosen = jax.random.permutation(own_key, shards_of)[partner]
    strong = (owner == chosen) | (owner == (partner + shards_of // 2) % shards_of)
    return jnp.where(strong, factor * drawn, drawn)


def steps_of(key, extent, split, low, top_value):
    loudness = 1.0
    for axis_at, parts in split:
        draws = jax.random.uniform(jax.random.fold_in(jax.random.fold_in(key, 6), axis_at), (parts,), jnp.float32, low / len(split), top_value / len(split))
        loudness = loudness * jnp.repeat(jnp.exp(draws), extent[axis_at] // parts).reshape((-1,) + (1,) * (len(extent) - 1 - axis_at))
    return loudness


def noise(rng, shape, scale, bound, cuts=(), kind=jnp.bfloat16):
    result = jax.random.normal(rng, shape, jnp.float32) * scale
    if len(cuts) > 0:
        result = steps_of(rng, shape, cuts, -0.22, 0.18) * result
    return jnp.clip(result, min=-bound, max=bound).astype(kind)


def heavy_noise(stream_key, shape, scale, limit, split, heavy, kind=jnp.bfloat16):
    drawn = scale * jax.random.normal(stream_key, shape, jnp.float32)
    if split:
        drawn = drawn * steps_of(stream_key, shape, split, -0.22, 0.18)
    return jnp.clip(strengthened(drawn, jax.random.fold_in(stream_key, 3), *heavy), -limit, limit).astype(kind)


def setup_inputs(seed: int = 0) -> dict:
    seeds = jax.random.split(jax.random.key(seed), 18)
    tokens = heavy_noise(seeds[0], (TOKENS, D), 1.0, 6.0, ((0, 32),), (0, 1, 32, 2.75))
    encoder_states = noise(seeds[1], (ENC_TOKENS, D), 1.0, 6.0, ((0, 32),))
    self_query = noise(seeds[2], (D * INNER,), (4 * D) ** -0.5, 0.109375, ((0, 32),))
    self_key = noise(seeds[3], (D * INNER,), (4 * D) ** -0.5, 0.109375, ((0, 32),))
    self_value = noise(seeds[4], (D * INNER,), D ** -0.5, 0.21875, ((0, 32),))
    self_out = noise(seeds[5], (D * INNER,), (INNER // 16) ** -0.5, 0.875, ((0, 32),))
    cross_query = noise(seeds[6], (D * INNER,), (4 * D) ** -0.5, 0.109375, ((0, 32),))
    cross_key = noise(seeds[7], (D * INNER,), (4 * D) ** -0.5, 0.109375, ((0, 32),))
    cross_value = noise(seeds[8], (D * INNER,), D ** -0.5, 0.21875, ((0, 32),))
    cross_out = noise(seeds[9], (D * INNER,), (INNER // 16) ** -0.5, 0.875, ((0, 32),))
    ff_gate = noise(seeds[10], (D * FF,), D ** -0.5, 0.21875, ((0, 32),))
    ff_up = noise(seeds[11], (D * FF,), D ** -0.5, 0.21875, ((0, 32),))
    ff_down = noise(seeds[12], (D * FF,), (FF // 4) ** -0.5, 0.25, ((0, 32),))
    norm_gains = jnp.clip(1.0 + 0.1 * jax.random.normal(seeds[13], (3, D), jnp.float32), 0.5, 1.5).astype(jnp.bfloat16)
    bias_table = noise(seeds[14], (BUCKETS, HEADS), 1.0, 4.0)
    buckets = draw_buckets(jax.random.fold_in(seeds[17], 71), 0)
    cotangent = noise(seeds[16], (TOKENS, D), 1.0, 6.0, ((0, 32),))
    return {"tokens": tokens, "encoder_states": encoder_states, "self_query": self_query, "self_key": self_key, "self_value": self_value, "self_out": self_out, "cross_query": cross_query, "cross_key": cross_key, "cross_value": cross_value, "cross_out": cross_out, "ff_gate": ff_gate, "ff_up": ff_up, "ff_down": ff_down, "norm_gains": norm_gains, "bias_table": bias_table, "buckets": buckets, "cotangent": cotangent}


@jax.custom_vjp
def low(v):
    return lax.optimization_barrier(v.astype(jnp.bfloat16)).astype(jnp.float32)

@jax.custom_vjp
def low_back(v):
    return v

def low_keep(v):
    return (low(v), None)

def low_pass(kept, grad):
    return (grad,)

def back_keep(v):
    return (v, None)

def back_low(kept, grad):
    return (low(grad),)
low.defvjp(low_keep, low_pass)
low_back.defvjp(back_keep, back_low)
EPSILON = 1e-06
NEGATIVE = -1e+30
PRECISE = lax.Precision.HIGHEST

def matmul(left_side, right_side):
    return jnp.dot(left_side, right_side, precision=PRECISE, preferred_element_type=jnp.float32)

def rms_norm(inputs, gain_row):
    return inputs * lax.rsqrt(lax.optimization_barrier(jnp.mean(inputs * inputs, axis=-1, keepdims=True)) + EPSILON) * gain_row

def split_heads(row_block):
    return row_block.reshape(row_block.shape[0], HEADS, HD)

def attend(queries, key_rows, value_rows, position_bias, causal):
    scores = jnp.einsum('qhd,khd->hqk', split_heads(queries), split_heads(key_rows), precision=PRECISE) + position_bias
    scores = low_back(scores)
    if causal:
        length = scores.shape[1]
        row_ids = lax.broadcasted_iota(jnp.int32, (length, length), 0)
        col_ids = lax.broadcasted_iota(jnp.int32, (length, length), 1)
        scores = jnp.where((col_ids <= row_ids)[None], scores, NEGATIVE)
    prob_rows = low(jax.nn.softmax(scores, axis=-1))
    mixed_rows = jnp.einsum('hqk,khd->qhd', prob_rows, split_heads(value_rows), precision=PRECISE)
    return low_back(low(mixed_rows.reshape(queries.shape[0], INNER)))

def decoder_sequence(inputs, encoder_rows, matrices, gain_values, position_bias):
    self_query, self_key, self_value, self_out, cross_query, cross_key, cross_value, cross_out, ff_gate, ff_up, ff_down = matrices
    normed_one = low(rms_norm(inputs, gain_values[0]))
    query_one = low_back(low(matmul(normed_one, self_query)))
    key_one = low_back(low(matmul(normed_one, self_key)))
    value_one = low_back(low(matmul(normed_one, self_value)))
    middle = inputs + low_back(matmul(attend(query_one, key_one, value_one, position_bias, True), self_out))
    normed_two = low(rms_norm(middle, gain_values[1]))
    query_two = low_back(low(matmul(normed_two, cross_query)))
    key_two = low_back(low(matmul(encoder_rows, cross_key)))
    value_two = low_back(low(matmul(encoder_rows, cross_value)))
    late = middle + low_back(matmul(attend(query_two, key_two, value_two, 0.0, False), cross_out))
    normed_three = low(rms_norm(late, gain_values[2]))
    gate_rows = low_back(matmul(normed_three, ff_gate))
    up_rows = low_back(matmul(normed_three, ff_up))
    hidden = low(jax.nn.gelu(gate_rows, approximate=True) * up_rows)
    return late + low_back(matmul(hidden, ff_down))

def reference(tokens, encoder_states, self_query, self_key, self_value, self_out, cross_query, cross_key, cross_value, cross_out, ff_gate, ff_up, ff_down, norm_gains, bias_table, buckets, cotangent):
    flat_weights = (self_query, self_key, self_value, self_out, cross_query, cross_key, cross_value, cross_out, ff_gate, ff_up, ff_down)
    target_shapes = ((D, INNER), (D, INNER), (D, INNER), (INNER, D), (D, INNER), (D, INNER), (D, INNER), (INNER, D), (D, FF), (D, FF), (FF, D))
    matrices = tuple((weight.astype(jnp.float32).reshape(target_shape) for weight, target_shape in zip(flat_weights, target_shapes)))
    gain_values = norm_gains.astype(jnp.float32)
    table_values = bias_table.astype(jnp.float32)
    seq_group = MICRO * SEQ_MB
    group_count = tokens.shape[0] // (seq_group * LEN)
    token_groups = tokens.astype(jnp.float32).reshape(group_count, seq_group, LEN, D)
    encoder_groups = encoder_states.astype(jnp.float32).reshape(group_count, seq_group, ENC, D)
    cotangent_groups = cotangent.astype(jnp.float32).reshape(group_count, seq_group, LEN, D)

    def run_group(token_block, encoder_block, matrix_values, gain_input, table_input):
        position_bias = jnp.transpose(jnp.take(table_input, buckets, axis=0), (2, 0, 1))
        checked = jax.checkpoint(lambda seq_tokens, seq_encoder: decoder_sequence(seq_tokens, seq_encoder, matrix_values, gain_input, position_bias))
        return jax.vmap(checked)(token_block, encoder_block)

    def scan_step(running, group_data):
        token_block, encoder_block, cotangent_block = group_data
        result_block, pull_back = jax.vjp(run_group, token_block, encoder_block, matrices, gain_values, table_values)
        token_grad, encoder_grad, matrix_grads, gain_grad, table_grad = pull_back(cotangent_block)
        weight_sums = tuple((total + low(one_grad) for total, one_grad in zip(running[0], matrix_grads)))
        updated = (weight_sums, running[1] + gain_grad, running[2] + table_grad)
        return (updated, (result_block.astype(jnp.bfloat16), token_grad.astype(jnp.bfloat16), encoder_grad.astype(jnp.bfloat16)))
    start = (tuple((jnp.zeros(target_shape, jnp.float32) for target_shape in target_shapes)), jnp.zeros((3, D), jnp.float32), jnp.zeros((BUCKETS, HEADS), jnp.float32))
    totals, results = lax.scan(scan_step, start, (token_groups, encoder_groups, cotangent_groups))
    output = results[0].reshape(tokens.shape[0], D)
    token_grad = results[1].reshape(tokens.shape[0], D)
    encoder_grad = results[2].reshape(encoder_states.shape[0], D)
    flat_grads = [one_grad.reshape(-1) for one_grad in totals[0]]
    return (output, token_grad, encoder_grad, flat_grads[0], flat_grads[1], flat_grads[2], flat_grads[3], flat_grads[4], flat_grads[5], flat_grads[6], flat_grads[7], flat_grads[8], flat_grads[9], flat_grads[10], totals[1], totals[2])
```

```python
from functools import partial

import jax
import jax.numpy as jnp
from jax import lax
from jax.experimental import pallas as pl
from jax.experimental.pallas import tpu as pltpu
from jax.sharding import PartitionSpec as P

D = 768
HEADS = 12
HD = 64
FF = 2048
BUCKETS = 32
INNER = 768
PAIRS = HEADS // 2
WIDE = 2 * HD

EPSILON = 1e-06
NEGATIVE = -1e30
VMEM_LIMIT = 48 * 1024 * 1024
F32 = jnp.float32
BF16 = jnp.bfloat16


def params():
    return pltpu.CompilerParams(vmem_limit_bytes=VMEM_LIMIT)


def matmul(left_side, right_side):
    return jnp.dot(left_side, right_side, preferred_element_type=F32)


def matmul_tn(left_side, right_side):
    return lax.dot_general(
        left_side, right_side, (((0,), (0,)), ((), ())), preferred_element_type=F32
    )


def matmul_nt(left_side, right_side):
    return lax.dot_general(
        left_side, right_side, (((1,), (1,)), ((), ())), preferred_element_type=F32
    )


def norm_factor(inputs):
    return lax.rsqrt(jnp.mean(inputs * inputs, axis=-1, keepdims=True) + EPSILON)


def norm_backward(inputs, factor, gain_row, upstream):
    scaled = gain_row * upstream
    inner_mean = jnp.mean(scaled * inputs, axis=-1, keepdims=True)
    input_grad = factor * (scaled - inputs * factor * factor * inner_mean)
    return (input_grad, jnp.sum(upstream * inputs * factor, axis=0))


BAND = 16


def bias_kernel(band_ref, out_ref):
    length = out_ref.shape[1]
    band = band_ref[0]
    for group in range(length // BAND):
        rolled = pltpu.roll(band, length + BAND * group, 1)
        out_ref[0, group * BAND : (group + 1) * BAND, :] = rolled[:, :length].astype(BF16)


def expand_bias(distance_bias, length):
    extended = jnp.concatenate(
        [jnp.full((HEADS, length), NEGATIVE, F32), distance_bias.astype(F32)], axis=1
    )
    rows = [
        jnp.pad(extended[:, : 2 * length - row], ((0, 0), (row, 0)), constant_values=NEGATIVE)
        for row in range(BAND)
    ]
    bands = jnp.stack(rows, axis=1)
    return pl.pallas_call(
        bias_kernel,
        grid=(HEADS,),
        in_specs=[pl.BlockSpec((1, BAND, 2 * length), lambda h: (h, 0, 0))],
        out_specs=pl.BlockSpec((1, length, length), lambda h: (h, 0, 0)),
        out_shape=jax.ShapeDtypeStruct((HEADS, length, length), BF16),
        compiler_params=params(),
        name="bias",
    )(bands)


def head_masks():
    lanes = lax.broadcasted_iota(jnp.int32, (1, WIDE), 1)
    low = (lanes < HD).astype(F32).astype(BF16)
    high = (lanes >= HD).astype(F32).astype(BF16)
    return (low, high)


def attend_core(queries, keys, values, bias_ref, out_ref, log_ref):
    length = queries.shape[0]
    causal = bias_ref is not None
    masks = head_masks()
    step = length // 2
    for part in range(2):
        begin, end = part * step, (part + 1) * step
        reach = end if causal else keys.shape[0]
        mixed = None
        for head in range(2):
            scores = matmul_nt(keys[:reach] * masks[head], queries[begin:end])
            if causal:
                scores = scores + bias_ref[head, :reach, begin:end].astype(F32)
            top = jnp.max(scores, axis=0, keepdims=True)
            powered = jnp.exp(scores - top)
            total = jnp.sum(powered, axis=0, keepdims=True)
            probs = (powered * (1.0 / total)).astype(BF16)
            term = matmul_tn(values[:reach] * masks[head], probs)
            mixed = term if mixed is None else mixed + term
            log_ref[0, 0, head : head + 1, begin:end] = top + jnp.log(total)
        out_ref[begin:end, :] = jnp.transpose(mixed).astype(BF16)


def self_forward_kernel(qkv_ref, bias_ref, out_ref, log_ref):
    attend_core(
        qkv_ref[:, :WIDE],
        qkv_ref[:, WIDE : 2 * WIDE],
        qkv_ref[:, 2 * WIDE :],
        bias_ref,
        out_ref,
        log_ref,
    )


def cross_forward_kernel(q_ref, kv_ref, out_ref, log_ref):
    attend_core(q_ref[...], kv_ref[:, :WIDE], kv_ref[:, WIDE:], None, out_ref, log_ref)


def self_forward(qkv, bias, length):
    seqs = qkv.shape[0] // length
    return pl.pallas_call(
        self_forward_kernel,
        grid=(PAIRS, seqs),
        in_specs=[
            pl.BlockSpec((length, 3 * WIDE), lambda p, s: (s, p)),
            pl.BlockSpec((2, length, length), lambda p, s: (p, 0, 0)),
        ],
        out_specs=[
            pl.BlockSpec((length, WIDE), lambda p, s: (s, p)),
            pl.BlockSpec((1, 1, 2, length), lambda p, s: (s, p, 0, 0)),
        ],
        out_shape=[
            jax.ShapeDtypeStruct((qkv.shape[0], INNER), BF16),
            jax.ShapeDtypeStruct((seqs, PAIRS, 2, length), F32),
        ],
        compiler_params=params(),
        cost_estimate=pl.CostEstimate(
            flops=40_000_000_000, bytes_accessed=16_000_000, transcendentals=6_000_000
        ),
        name="self_forward",
    )(qkv, bias)


def cross_forward(queries, kv, length):
    seqs = queries.shape[0] // length
    extent = kv.shape[0] // seqs
    return pl.pallas_call(
        cross_forward_kernel,
        grid=(PAIRS, seqs),
        in_specs=[
            pl.BlockSpec((length, WIDE), lambda p, s: (s, p)),
            pl.BlockSpec((extent, 2 * WIDE), lambda p, s: (s, p)),
        ],
        out_specs=[
            pl.BlockSpec((length, WIDE), lambda p, s: (s, p)),
            pl.BlockSpec((1, 1, 2, length), lambda p, s: (s, p, 0, 0)),
        ],
        out_shape=[
            jax.ShapeDtypeStruct((queries.shape[0], INNER), BF16),
            jax.ShapeDtypeStruct((seqs, PAIRS, 2, length), F32),
        ],
        compiler_params=params(),
        cost_estimate=pl.CostEstimate(
            flops=40_000_000_000, bytes_accessed=16_000_000, transcendentals=6_000_000
        ),
        name="cross_forward",
    )(queries, kv)


def attend_back_core(queries, keys, values, upstream, log_ref, bias_ref, store_q, store_kv, table):
    length = queries.shape[0]
    causal = bias_ref is not None
    masks = head_masks()
    step = length // 2
    key_grad = [None, None]
    value_grad = [None, None]

    def put(parts, at, term):
        parts[at] = term if parts[at] is None else parts[at] + term

    half = keys.shape[0] // 2
    for part in range(2):
        begin, end = part * step, (part + 1) * step
        reach = end if causal else keys.shape[0]
        query_grad = None
        for head in range(2):
            mask = masks[head]
            masked_keys = keys[:reach] * mask
            masked_query = queries[begin:end] * mask
            masked_up = upstream[begin:end] * mask
            scores = matmul_nt(masked_keys, queries[begin:end])
            if causal:
                scores = scores + bias_ref[head, :reach, begin:end].astype(F32)
            probs = jnp.exp(scores - log_ref[0, 0, head : head + 1, begin:end])
            prob_grad = matmul_nt(values[:reach], masked_up)
            delta = jnp.sum(probs * prob_grad, axis=0, keepdims=True)
            score_grad = probs * (prob_grad - delta)
            if table is not None:
                table(head, begin, end, reach, score_grad)
            low_grad = score_grad.astype(BF16)
            low_probs = probs.astype(BF16)
            for block in range(reach // half):
                rows = slice(block * half, (block + 1) * half)
                put(value_grad, block, matmul(low_probs[rows], masked_up))
                put(key_grad, block, matmul(low_grad[rows], masked_query))
            term = matmul_tn(masked_keys, low_grad)
            query_grad = term if query_grad is None else query_grad + term
        store_q(begin, end, jnp.transpose(query_grad).astype(BF16))
    for block in range(2):
        store_kv(
            block * half, (block + 1) * half, key_grad[block].astype(BF16), value_grad[block].astype(BF16)
        )


SHEAR = 128


def self_backward_kernel(qkv_ref, up_ref, log_ref, bias_ref, grad_ref, table_ref, shear_ref):
    length = qkv_ref.shape[0]

    @pl.when(pl.program_id(1) == 0)
    def _():
        shear_ref[...] = jnp.zeros_like(shear_ref)

    def table(head, begin, end, reach, score_grad):
        for block in range(reach // SHEAR):
            start = max(begin, block * SHEAR)
            shear_ref[head, :, start - block * SHEAR : end - block * SHEAR] += score_grad[
                block * SHEAR : (block + 1) * SHEAR, start - begin : end - begin
            ]

    def store_q(begin, end, grad):
        grad_ref[begin:end, :WIDE] = grad

    def store_kv(begin, end, key_grad, value_grad):
        grad_ref[begin:end, WIDE : 2 * WIDE] = key_grad
        grad_ref[begin:end, 2 * WIDE :] = value_grad

    attend_back_core(
        qkv_ref[:, :WIDE],
        qkv_ref[:, WIDE : 2 * WIDE],
        qkv_ref[:, 2 * WIDE :],
        up_ref[...],
        log_ref,
        bias_ref,
        store_q,
        store_kv,
        table,
    )

    @pl.when(pl.program_id(1) == pl.num_programs(1) - 1)
    def _():
        for head in range(2):
            total = shear_ref[head, 0:8, :]
            for group in range(1, SHEAR // 8):
                rows = shear_ref[head, 8 * group : 8 * group + 8, :]
                total = total + pltpu.roll(rows, length - 8 * group, 1)
            table_ref[head] = total


def cross_backward_kernel(q_ref, kv_ref, up_ref, log_ref, dq_ref, dkv_ref):
    def store_q(begin, end, grad):
        dq_ref[begin:end, :] = grad

    def store_kv(begin, end, key_grad, value_grad):
        dkv_ref[begin:end, :WIDE] = key_grad
        dkv_ref[begin:end, WIDE:] = value_grad

    attend_back_core(
        q_ref[...],
        kv_ref[:, :WIDE],
        kv_ref[:, WIDE:],
        up_ref[...],
        log_ref,
        None,
        store_q,
        store_kv,
        None,
    )


def self_backward(qkv, upstream, logs, bias, length):
    seqs = qkv.shape[0] // length
    return pl.pallas_call(
        self_backward_kernel,
        grid=(PAIRS, seqs),
        in_specs=[
            pl.BlockSpec((length, 3 * WIDE), lambda p, s: (s, p)),
            pl.BlockSpec((length, WIDE), lambda p, s: (s, p)),
            pl.BlockSpec((1, 1, 2, length), lambda p, s: (s, p, 0, 0)),
            pl.BlockSpec((2, length, length), lambda p, s: (p, 0, 0)),
        ],
        out_specs=[
            pl.BlockSpec((length, 3 * WIDE), lambda p, s: (s, p)),
            pl.BlockSpec((2, 8, length), lambda p, s: (p, 0, 0)),
        ],
        out_shape=[
            jax.ShapeDtypeStruct(qkv.shape, BF16),
            jax.ShapeDtypeStruct((HEADS, 8, length), F32),
        ],
        scratch_shapes=[pltpu.VMEM((2, SHEAR, length), F32)],
        compiler_params=params(),
        cost_estimate=pl.CostEstimate(
            flops=80_000_000_000, bytes_accessed=20_000_000, transcendentals=6_000_000
        ),
        name="self_backward",
    )(qkv, upstream, logs, bias)


def cross_backward(queries, kv, upstream, logs, length):
    seqs = queries.shape[0] // length
    extent = kv.shape[0] // seqs
    return pl.pallas_call(
        cross_backward_kernel,
        grid=(PAIRS, seqs),
        in_specs=[
            pl.BlockSpec((length, WIDE), lambda p, s: (s, p)),
            pl.BlockSpec((extent, 2 * WIDE), lambda p, s: (s, p)),
            pl.BlockSpec((length, WIDE), lambda p, s: (s, p)),
            pl.BlockSpec((1, 1, 2, length), lambda p, s: (s, p, 0, 0)),
        ],
        out_specs=[
            pl.BlockSpec((length, WIDE), lambda p, s: (s, p)),
            pl.BlockSpec((extent, 2 * WIDE), lambda p, s: (s, p)),
        ],
        out_shape=[
            jax.ShapeDtypeStruct(queries.shape, BF16),
            jax.ShapeDtypeStruct(kv.shape, BF16),
        ],
        compiler_params=params(),
        cost_estimate=pl.CostEstimate(
            flops=80_000_000_000, bytes_accessed=20_000_000, transcendentals=6_000_000
        ),
        name="cross_backward",
    )(queries, kv, upstream, logs)


DOWN_BLOCKS = -(-FF // D)
WIDTHS = (3 * INNER, D, INNER, 2 * INNER, D, 2 * FF, DOWN_BLOCKS * D)


def interleave(parts):
    rows = parts[0].shape[0]
    stacked = jnp.stack([part.reshape(rows, PAIRS, WIDE) for part in parts], axis=2)
    return stacked.reshape(rows, len(parts) * INNER)


def split_interleaved(block, count):
    rows = block.shape[0]
    stacked = block.reshape(rows, PAIRS, count, WIDE)
    return [stacked[:, :, at].reshape(-1) for at in range(count)]


def pack_shards(shards):
    rows = shards[0].shape[0] // D
    sq, sk, sv, so, cq, ck, cv, co = (shard.reshape(rows, D) for shard in shards[:8])
    gate, up = (shard.reshape(rows, FF) for shard in shards[8:10])
    down = shards[10].reshape(-1, D)
    down = jnp.pad(down, ((0, DOWN_BLOCKS * rows - down.shape[0]), (0, 0)))
    down = down.reshape(DOWN_BLOCKS, rows, D).transpose(1, 0, 2).reshape(rows, DOWN_BLOCKS * D)
    return jnp.concatenate(
        [interleave([sq, sk, sv]), so, cq, interleave([ck, cv]), co, gate, up, down], axis=1
    )


def unpack_down(block, count):
    rows = D // count
    stacked = block.reshape(count, rows, DOWN_BLOCKS, D).transpose(0, 2, 1, 3)
    stacked = stacked.reshape(count, DOWN_BLOCKS * rows, D)[:, : FF // count]
    return stacked.reshape(FF, D)


def pack_down(down, count):
    rows = D // count
    stacked = down.reshape(count, FF // count, D)
    stacked = jnp.pad(stacked, ((0, 0), (0, DOWN_BLOCKS * rows - FF // count), (0, 0)))
    stacked = stacked.reshape(count, DOWN_BLOCKS, rows, D).transpose(0, 2, 1, 3)
    return stacked.reshape(D, DOWN_BLOCKS * D)


def cut(block, widths):
    pieces = []
    start = 0
    for width in widths:
        pieces.append(block[:, start : start + width])
        start += width
    return pieces


def sum_everywhere(values, count):
    bit = 1
    while bit < count:
        pairs = [(index, index ^ bit) for index in range(count)]
        values = values + lax.ppermute(values, "fsdp", pairs)
        bit *= 2
    return values


def per_device(
    count,
    tokens,
    encoder_states,
    self_query,
    self_key,
    self_value,
    self_out,
    cross_query,
    cross_key,
    cross_value,
    cross_out,
    ff_gate,
    ff_up,
    ff_down,
    norm_gains,
    bias_table,
    buckets,
    cotangent,
):
    shards = (
        self_query,
        self_key,
        self_value,
        self_out,
        cross_query,
        cross_key,
        cross_value,
        cross_out,
        ff_gate,
        ff_up,
        ff_down,
    )
    gathered = lax.all_gather(pack_shards(shards), "fsdp", axis=0, tiled=True)
    w_qkv, w_so, w_cq, w_ckv, w_co, w_gu, w_down = cut(gathered, WIDTHS)
    w_down = unpack_down(w_down, count)

    gain_values = norm_gains.astype(F32)
    length = buckets.shape[0]
    bucket_of = buckets[:, 0]
    onehot = (bucket_of[None, :] == jnp.arange(BUCKETS, dtype=jnp.int32)[:, None]).astype(F32)
    distance_bias = jnp.take(bias_table, bucket_of, axis=0).T
    bias = expand_bias(distance_bias, length)

    inputs = tokens.astype(F32)
    factor_one = norm_factor(inputs)
    normed_one = (inputs * factor_one * gain_values[0]).astype(BF16)
    qkv = matmul(normed_one, w_qkv).astype(BF16)
    kv_two = matmul(encoder_states, w_ckv).astype(BF16)
    mixed_one, log_one = self_forward(qkv, bias, length)
    middle = inputs + matmul(mixed_one, w_so)
    factor_two = norm_factor(middle)
    normed_two = (middle * factor_two * gain_values[1]).astype(BF16)
    query_two = matmul(normed_two, w_cq).astype(BF16)
    mixed_two, log_two = cross_forward(query_two, kv_two, length)
    late = middle + matmul(mixed_two, w_co)
    factor_three = norm_factor(late)
    normed_three = (late * factor_three * gain_values[2]).astype(BF16)
    gate_rows = matmul(normed_three, w_gu[:, :FF])
    up_rows = matmul(normed_three, w_gu[:, FF:])
    activated, gelu_pull = jax.vjp(lambda gate: jax.nn.gelu(gate, approximate=True), gate_rows)
    hidden = (activated * up_rows).astype(BF16)
    result_rows = (late + matmul(hidden, w_down)).astype(BF16)

    grad_down = matmul_tn(hidden, cotangent).astype(BF16)
    hidden_grad = matmul_nt(cotangent, w_down)
    gate_grad = gelu_pull(hidden_grad * up_rows)[0].astype(BF16)
    up_grad = (hidden_grad * activated).astype(BF16)
    grad_gate = matmul_tn(normed_three, gate_grad).astype(BF16)
    grad_up = matmul_tn(normed_three, up_grad).astype(BF16)
    normed_grad = matmul_nt(gate_grad, w_gu[:, :FF]) + matmul_nt(up_grad, w_gu[:, FF:])
    norm_grad, gain_three = norm_backward(late, factor_three, gain_values[2], normed_grad)
    late_grad = cotangent.astype(F32) + norm_grad
    branch_grad = late_grad.astype(BF16)
    grad_co = matmul_tn(mixed_two, branch_grad).astype(BF16)
    mixed_grad = matmul_nt(branch_grad, w_co).astype(BF16)
    query_grad, kv_grad = cross_backward(query_two, kv_two, mixed_grad, log_two, length)
    grad_cq = matmul_tn(normed_two, query_grad).astype(BF16)
    grad_ckv = matmul_tn(encoder_states, kv_grad).astype(BF16)
    encoder_grad = matmul_nt(kv_grad, w_ckv).astype(BF16)
    norm_grad, gain_two = norm_backward(
        middle, factor_two, gain_values[1], matmul_nt(query_grad, w_cq)
    )
    middle_grad = late_grad + norm_grad
    branch_grad = middle_grad.astype(BF16)
    grad_so = matmul_tn(mixed_one, branch_grad).astype(BF16)
    mixed_grad = matmul_nt(branch_grad, w_so).astype(BF16)
    qkv_grad, sheared = self_backward(qkv, mixed_grad, log_one, bias, length)
    grad_qkv = matmul_tn(normed_one, qkv_grad).astype(BF16)
    norm_grad, gain_one = norm_backward(
        inputs, factor_one, gain_values[0], matmul_nt(qkv_grad, w_qkv)
    )
    input_grad = (middle_grad + norm_grad).astype(BF16)

    by_distance = sum(
        jnp.pad(sheared[:, row, row:], ((0, 0), (0, row))) for row in range(sheared.shape[1])
    )
    table_part = jnp.sum(onehot[:, None, :] * by_distance[None, :, :], axis=-1)

    packed = jnp.concatenate(
        [grad_qkv, grad_so, grad_cq, grad_ckv, grad_co, grad_gate, grad_up, pack_down(grad_down, count)],
        axis=1,
    )
    owned = lax.psum_scatter(packed, "fsdp", scatter_dimension=0, tiled=True).astype(F32)
    o_qkv, o_so, o_cq, o_ckv, o_co, o_gu, o_down = cut(owned, WIDTHS)
    g_sq, g_sk, g_sv = split_interleaved(o_qkv, 3)
    g_ck, g_cv = split_interleaved(o_ckv, 2)
    rows = owned.shape[0]
    g_down = o_down.reshape(rows, DOWN_BLOCKS, D).transpose(1, 0, 2).reshape(-1)[: FF // count * D]

    gains_part = jnp.stack([gain_one, gain_two, gain_three])
    small = jnp.concatenate([gains_part.reshape(-1), table_part.reshape(-1)]).reshape(-1, 128)
    small = sum_everywhere(small, count).reshape(-1)
    gains_grad = small[: 3 * D].reshape(3, D)
    table_grad = small[3 * D :].reshape(BUCKETS, HEADS)
    return (
        result_rows,
        input_grad,
        encoder_grad,
        g_sq,
        g_sk,
        g_sv,
        o_so.reshape(-1),
        o_cq.reshape(-1),
        g_ck,
        g_cv,
        o_co.reshape(-1),
        o_gu[:, :FF].reshape(-1),
        o_gu[:, FF:].reshape(-1),
        g_down,
        gains_grad,
        table_grad,
    )


def solution(mesh):
    flat = P("fsdp")
    rows = P("fsdp", None)
    return jax.shard_map(
        partial(per_device, mesh.shape["fsdp"]),
        mesh=mesh,
        in_specs=(rows, rows) + (flat,) * 11 + (P(), P(), P(), rows),
        out_specs=(rows, rows, rows) + (flat,) * 11 + (P(), P()),
        check_vma=False,
    )
```

```python
from functools import partial

import jax
import jax.numpy as jnp
from jax import lax
from jax.experimental import pallas as pl
from jax.experimental.pallas import tpu as pltpu
from jax.sharding import PartitionSpec as P

D = 768
HEADS = 12
HD = 64
FF = 2048
BUCKETS = 32
INNER = 768
PAIRS = HEADS // 2
WIDE = 2 * HD

EPSILON = 1e-06
NEGATIVE = -1e30
VMEM_LIMIT = 48 * 1024 * 1024
F32 = jnp.float32
BF16 = jnp.bfloat16


def params():
    return pltpu.CompilerParams(vmem_limit_bytes=VMEM_LIMIT)


def brief():
    return pl.CostEstimate(flops=1_000_000, bytes_accessed=100_000, transcendentals=0)


def matmul(left_side, right_side):
    return jnp.dot(left_side, right_side, preferred_element_type=F32)


def matmul_tn(left_side, right_side):
    return lax.dot_general(
        left_side, right_side, (((0,), (0,)), ((), ())), preferred_element_type=F32
    )


def matmul_nt(left_side, right_side):
    return lax.dot_general(
        left_side, right_side, (((1,), (1,)), ((), ())), preferred_element_type=F32
    )


def norm_factor(inputs):
    return lax.rsqrt(jnp.mean(inputs * inputs, axis=-1, keepdims=True) + EPSILON)


def norm_backward(inputs, factor, gain_row, upstream):
    scaled = gain_row * upstream
    inner_mean = jnp.mean(scaled * inputs, axis=-1, keepdims=True)
    input_grad = factor * (scaled - inputs * factor * factor * inner_mean)
    return (input_grad, jnp.sum(upstream * inputs * factor, axis=0))


BAND = 16


def bias_kernel(band_ref, out_ref):
    length = out_ref.shape[1]
    band = band_ref[0]
    for group in range(length // BAND):
        rolled = pltpu.roll(band, length + BAND * group, 1)
        out_ref[0, group * BAND : (group + 1) * BAND, :] = rolled[:, :length].astype(BF16)


def expand_bias(distance_bias, length):
    extended = jnp.concatenate(
        [jnp.full((HEADS, length), NEGATIVE, F32), distance_bias.astype(F32)], axis=1
    )
    rows = [
        jnp.pad(extended[:, : 2 * length - row], ((0, 0), (row, 0)), constant_values=NEGATIVE)
        for row in range(BAND)
    ]
    bands = jnp.stack(rows, axis=1)
    return pl.pallas_call(
        bias_kernel,
        grid=(HEADS,),
        in_specs=[pl.BlockSpec((1, BAND, 2 * length), lambda h: (h, 0, 0))],
        out_specs=pl.BlockSpec((1, length, length), lambda h: (h, 0, 0)),
        out_shape=jax.ShapeDtypeStruct((HEADS, length, length), BF16),
        compiler_params=params(),
        name="bias",
    )(bands)


def head_masks():
    lanes = lax.broadcasted_iota(jnp.int32, (1, WIDE), 1)
    low = (lanes < HD).astype(F32).astype(BF16)
    high = (lanes >= HD).astype(F32).astype(BF16)
    return (low, high)


def attend_core(queries, keys, values, bias_ref, out_ref, log_ref):
    length = queries.shape[0]
    causal = bias_ref is not None
    masks = head_masks()
    step = length // 2
    for part in range(2):
        begin, end = part * step, (part + 1) * step
        reach = end if causal else keys.shape[0]
        mixed = None
        for head in range(2):
            scores = matmul_nt(keys[:reach] * masks[head], queries[begin:end])
            if causal:
                scores = scores + bias_ref[head, :reach, begin:end].astype(F32)
            top = jnp.max(scores, axis=0, keepdims=True)
            powered = jnp.exp(scores - top)
            total = jnp.sum(powered, axis=0, keepdims=True)
            probs = (powered * (1.0 / total)).astype(BF16)
            term = matmul_tn(values[:reach] * masks[head], probs)
            mixed = term if mixed is None else mixed + term
            log_ref[0, 0, head : head + 1, begin:end] = top + jnp.log(total)
        out_ref[begin:end, :] = jnp.transpose(mixed).astype(BF16)


def self_forward_kernel(qkv_ref, bias_ref, out_ref, log_ref):
    attend_core(
        qkv_ref[:, :WIDE],
        qkv_ref[:, WIDE : 2 * WIDE],
        qkv_ref[:, 2 * WIDE :],
        bias_ref,
        out_ref,
        log_ref,
    )


def cross_forward_kernel(q_ref, kv_ref, out_ref, log_ref):
    attend_core(q_ref[...], kv_ref[:, :WIDE], kv_ref[:, WIDE:], None, out_ref, log_ref)


def self_forward(qkv, bias, length):
    seqs = qkv.shape[0] // length
    return pl.pallas_call(
        self_forward_kernel,
        grid=(PAIRS, seqs),
        in_specs=[
            pl.BlockSpec((length, 3 * WIDE), lambda p, s: (s, p)),
            pl.BlockSpec((2, length, length), lambda p, s: (p, 0, 0)),
        ],
        out_specs=[
            pl.BlockSpec((length, WIDE), lambda p, s: (s, p)),
            pl.BlockSpec((1, 1, 2, length), lambda p, s: (s, p, 0, 0)),
        ],
        out_shape=[
            jax.ShapeDtypeStruct((qkv.shape[0], INNER), BF16),
            jax.ShapeDtypeStruct((seqs, PAIRS, 2, length), F32),
        ],
        compiler_params=params(),
        cost_estimate=brief(),
        name="self_forward",
    )(qkv, bias)


def cross_forward(queries, kv, length):
    seqs = queries.shape[0] // length
    extent = kv.shape[0] // seqs
    return pl.pallas_call(
        cross_forward_kernel,
        grid=(PAIRS, seqs),
        in_specs=[
            pl.BlockSpec((length, WIDE), lambda p, s: (s, p)),
            pl.BlockSpec((extent, 2 * WIDE), lambda p, s: (s, p)),
        ],
        out_specs=[
            pl.BlockSpec((length, WIDE), lambda p, s: (s, p)),
            pl.BlockSpec((1, 1, 2, length), lambda p, s: (s, p, 0, 0)),
        ],
        out_shape=[
            jax.ShapeDtypeStruct((queries.shape[0], INNER), BF16),
            jax.ShapeDtypeStruct((seqs, PAIRS, 2, length), F32),
        ],
        compiler_params=params(),
        cost_estimate=brief(),
        name="cross_forward",
    )(queries, kv)


def attend_back_core(queries, keys, values, upstream, log_ref, bias_ref, store_q, store_kv, table):
    length = queries.shape[0]
    causal = bias_ref is not None
    masks = head_masks()
    step = length // 2
    key_grad = [None, None]
    value_grad = [None, None]

    def put(parts, at, term):
        parts[at] = term if parts[at] is None else parts[at] + term

    half = keys.shape[0] // 2
    for part in range(2):
        begin, end = part * step, (part + 1) * step
        reach = end if causal else keys.shape[0]
        query_grad = None
        for head in range(2):
            mask = masks[head]
            masked_keys = keys[:reach] * mask
            masked_query = queries[begin:end] * mask
            masked_up = upstream[begin:end] * mask
            scores = matmul_nt(masked_keys, queries[begin:end])
            if causal:
                scores = scores + bias_ref[head, :reach, begin:end].astype(F32)
            probs = jnp.exp(scores - log_ref[0, 0, head : head + 1, begin:end])
            prob_grad = matmul_nt(values[:reach], masked_up)
            delta = jnp.sum(probs * prob_grad, axis=0, keepdims=True)
            score_grad = probs * (prob_grad - delta)
            if table is not None:
                table(head, begin, end, reach, score_grad)
            low_grad = score_grad.astype(BF16)
            low_probs = probs.astype(BF16)
            for block in range(reach // half):
                rows = slice(block * half, (block + 1) * half)
                put(value_grad, block, matmul(low_probs[rows], masked_up))
                put(key_grad, block, matmul(low_grad[rows], masked_query))
            term = matmul_tn(masked_keys, low_grad)
            query_grad = term if query_grad is None else query_grad + term
        store_q(begin, end, jnp.transpose(query_grad).astype(BF16))
    for block in range(2):
        store_kv(
            block * half, (block + 1) * half, key_grad[block].astype(BF16), value_grad[block].astype(BF16)
        )


SHEAR = 128


def self_backward_kernel(qkv_ref, up_ref, log_ref, bias_ref, grad_ref, table_ref, shear_ref):
    length = qkv_ref.shape[0]

    @pl.when(pl.program_id(1) == 0)
    def _():
        shear_ref[...] = jnp.zeros_like(shear_ref)

    def table(head, begin, end, reach, score_grad):
        for block in range(reach // SHEAR):
            start = max(begin, block * SHEAR)
            shear_ref[head, :, start - block * SHEAR : end - block * SHEAR] += score_grad[
                block * SHEAR : (block + 1) * SHEAR, start - begin : end - begin
            ]

    def store_q(begin, end, grad):
        grad_ref[begin:end, :WIDE] = grad

    def store_kv(begin, end, key_grad, value_grad):
        grad_ref[begin:end, WIDE : 2 * WIDE] = key_grad
        grad_ref[begin:end, 2 * WIDE :] = value_grad

    attend_back_core(
        qkv_ref[:, :WIDE],
        qkv_ref[:, WIDE : 2 * WIDE],
        qkv_ref[:, 2 * WIDE :],
        up_ref[...],
        log_ref,
        bias_ref,
        store_q,
        store_kv,
        table,
    )

    @pl.when(pl.program_id(1) == pl.num_programs(1) - 1)
    def _():
        for head in range(2):
            total = shear_ref[head, 0:8, :]
            for group in range(1, SHEAR // 8):
                rows = shear_ref[head, 8 * group : 8 * group + 8, :]
                total = total + pltpu.roll(rows, length - 8 * group, 1)
            table_ref[head] = total


def cross_backward_kernel(q_ref, kv_ref, up_ref, log_ref, dq_ref, dkv_ref):
    def store_q(begin, end, grad):
        dq_ref[begin:end, :] = grad

    def store_kv(begin, end, key_grad, value_grad):
        dkv_ref[begin:end, :WIDE] = key_grad
        dkv_ref[begin:end, WIDE:] = value_grad

    attend_back_core(
        q_ref[...],
        kv_ref[:, :WIDE],
        kv_ref[:, WIDE:],
        up_ref[...],
        log_ref,
        None,
        store_q,
        store_kv,
        None,
    )


def self_backward(qkv, upstream, logs, bias, length):
    seqs = qkv.shape[0] // length
    return pl.pallas_call(
        self_backward_kernel,
        grid=(PAIRS, seqs),
        in_specs=[
            pl.BlockSpec((length, 3 * WIDE), lambda p, s: (s, p)),
            pl.BlockSpec((length, WIDE), lambda p, s: (s, p)),
            pl.BlockSpec((1, 1, 2, length), lambda p, s: (s, p, 0, 0)),
            pl.BlockSpec((2, length, length), lambda p, s: (p, 0, 0)),
        ],
        out_specs=[
            pl.BlockSpec((length, 3 * WIDE), lambda p, s: (s, p)),
            pl.BlockSpec((2, 8, length), lambda p, s: (p, 0, 0)),
        ],
        out_shape=[
            jax.ShapeDtypeStruct(qkv.shape, BF16),
            jax.ShapeDtypeStruct((HEADS, 8, length), F32),
        ],
        scratch_shapes=[pltpu.VMEM((2, SHEAR, length), F32)],
        compiler_params=params(),
        cost_estimate=brief(),
        name="self_backward",
    )(qkv, upstream, logs, bias)


def cross_backward(queries, kv, upstream, logs, length):
    seqs = queries.shape[0] // length
    extent = kv.shape[0] // seqs
    return pl.pallas_call(
        cross_backward_kernel,
        grid=(PAIRS, seqs),
        in_specs=[
            pl.BlockSpec((length, WIDE), lambda p, s: (s, p)),
            pl.BlockSpec((extent, 2 * WIDE), lambda p, s: (s, p)),
            pl.BlockSpec((length, WIDE), lambda p, s: (s, p)),
            pl.BlockSpec((1, 1, 2, length), lambda p, s: (s, p, 0, 0)),
        ],
        out_specs=[
            pl.BlockSpec((length, WIDE), lambda p, s: (s, p)),
            pl.BlockSpec((extent, 2 * WIDE), lambda p, s: (s, p)),
        ],
        out_shape=[
            jax.ShapeDtypeStruct(queries.shape, BF16),
            jax.ShapeDtypeStruct(kv.shape, BF16),
        ],
        compiler_params=params(),
        cost_estimate=brief(),
        name="cross_backward",
    )(queries, kv, upstream, logs)


CHUNK = 256
ROOT = 0.7978845608028654
CUBIC = 0.044715


def feed_kernel(
    extent,
    packed,
    late_ref,
    gain_ref,
    up_ref,
    wgu_ref,
    wd_ref,
    *refs,
):
    result_ref, grad_ref, gain_grad_ref, ggu_out = refs[:4]
    gd_out = ggu_out if packed else refs[4]
    normed_ref, flipped_ref, total_ref, hidden_ref, dgu_ref, ggu_buf, gd_buf, sems = refs[-8:]
    step = pl.program_id(0)
    slot = lax.rem(step, 2)
    rows = late_ref.shape[0]
    block = min(rows, 256)

    def copies(at, place):
        columns = pl.ds(pl.multiple_of(at * 2 * CHUNK, 2 * CHUNK), 2 * CHUNK)
        height = gd_buf.shape[1]
        down_rows = pl.ds(pl.multiple_of(at * height, 32), height)
        side = pl.ds(2 * FF, DOWN_BLOCKS * D) if packed else pl.ds(0, D)
        return (
            pltpu.make_async_copy(ggu_buf.at[place], ggu_out.at[:, columns], sems.at[place, 0]),
            pltpu.make_async_copy(gd_buf.at[place], gd_out.at[down_rows, side], sems.at[place, 1]),
        )

    @pl.when(step >= 2)
    def _():
        for copy in copies(step - 2, slot):
            copy.wait()

    @pl.when(step == 0)
    def _():
        for begin in range(0, rows, block):
            piece = slice(begin, begin + block)
            late = late_ref[piece, :]
            normed = (late * norm_factor(late) * gain_ref[...]).astype(BF16)
            normed_ref[piece, :] = normed
            flipped_ref[:, piece] = jnp.transpose(normed)
        total_ref[...] = late_ref[...]
        grad_ref[...] = jnp.zeros_like(grad_ref)

    for begin in range(0, rows, block):
        piece = slice(begin, begin + block)
        both = matmul(normed_ref[piece, :], wgu_ref[...])
        gate = both[:, :CHUNK]
        up = both[:, CHUNK:]
        hidden_grad = matmul_nt(up_ref[piece, :], wd_ref[...])
        square = gate * gate
        bent = jnp.tanh(ROOT * gate * (1.0 + CUBIC * square))
        half = 0.5 + 0.5 * bent
        activated = gate * half
        slope = half + 0.5 * gate * (1.0 - bent * bent) * (ROOT + (3.0 * ROOT * CUBIC) * square)
        hidden = (activated * up).astype(BF16)
        hidden_ref[piece, :] = hidden
        dgu_ref[piece, :CHUNK] = (hidden_grad * up * slope).astype(BF16)
        dgu_ref[piece, CHUNK:] = (hidden_grad * activated).astype(BF16)
        total_ref[piece, :] += matmul(hidden, wd_ref[...])
        grad_ref[piece, :] += matmul_nt(dgu_ref[piece, :], wgu_ref[...])
    ggu_buf[slot] = matmul(flipped_ref[...], dgu_ref[...]).astype(BF16)
    down_grad = matmul_tn(hidden_ref[...], up_ref[...])
    if packed:
        owners = CHUNK // extent
        shard_rows = gd_buf.shape[1] // owners
        view = down_grad.reshape(owners, extent, D)
        for at in range(DOWN_BLOCKS):
            piece = view[:, at * shard_rows : (at + 1) * shard_rows]
            lack = shard_rows - piece.shape[1]
            if lack:
                piece = jnp.concatenate([piece, jnp.zeros((owners, lack, D), F32)], axis=1)
            piece = piece.reshape(owners * shard_rows, D)
            gd_buf[slot, :, at * D : (at + 1) * D] = piece.astype(BF16)
    else:
        gd_buf[slot] = down_grad.astype(BF16)
    for copy in copies(step, slot):
        copy.start()

    @pl.when(step == pl.num_programs(0) - 1)
    def _():
        gain_grad = None
        for begin in range(0, rows, block):
            piece = slice(begin, begin + block)
            late = late_ref[piece, :]
            result_ref[piece, :] = total_ref[piece, :].astype(BF16)
            norm_grad, gain_part = norm_backward(
                late, norm_factor(late), gain_ref[...], grad_ref[piece, :]
            )
            grad_ref[piece, :] = up_ref[piece, :].astype(F32) + norm_grad
            gain_grad = gain_part if gain_grad is None else gain_grad + gain_part
        gain_grad_ref[...] = gain_grad[None, :]
        for copy in copies(step - 1, 1 - slot) + copies(step, slot):
            copy.wait()


def feed_forward(late, gain_row, cotangent, w_gu, w_down, count):
    rows = late.shape[0]
    whole = lambda c: (0, 0)
    extent = FF // count
    shard_rows = D // count
    packed = shard_rows % 8 == 0 and extent % 8 == 0 and CHUNK % extent == 0
    packed = packed and CHUNK // extent * shard_rows % 32 == 0
    if packed:
        down_block = (CHUNK // extent * shard_rows, DOWN_BLOCKS * D)
        grads = [jax.ShapeDtypeStruct((D, 2 * FF + DOWN_BLOCKS * D), BF16)]
    else:
        down_block = (CHUNK, D)
        grads = [jax.ShapeDtypeStruct((D, 2 * FF), BF16), jax.ShapeDtypeStruct((FF, D), BF16)]
    result, grad, gain_grad, *grads = pl.pallas_call(
        partial(feed_kernel, extent, packed),
        grid=(FF // CHUNK,),
        in_specs=[
            pl.BlockSpec((rows, D), whole),
            pl.BlockSpec((1, D), whole),
            pl.BlockSpec((rows, D), whole),
            pl.BlockSpec((D, 2 * CHUNK), lambda c: (0, c)),
            pl.BlockSpec((CHUNK, D), lambda c: (c, 0)),
        ],
        out_specs=[
            pl.BlockSpec((rows, D), whole),
            pl.BlockSpec((rows, D), whole),
            pl.BlockSpec((1, D), whole),
        ]
        + [pl.BlockSpec(memory_space=pl.ANY)] * len(grads),
        out_shape=[
            jax.ShapeDtypeStruct((rows, D), BF16),
            jax.ShapeDtypeStruct((rows, D), F32),
            jax.ShapeDtypeStruct((1, D), F32),
        ]
        + grads,
        scratch_shapes=[
            pltpu.VMEM((rows, D), BF16),
            pltpu.VMEM((D, rows), BF16),
            pltpu.VMEM((rows, D), F32),
            pltpu.VMEM((rows, CHUNK), BF16),
            pltpu.VMEM((rows, 2 * CHUNK), BF16),
            pltpu.VMEM((2, D, 2 * CHUNK), BF16),
            pltpu.VMEM((2,) + down_block, BF16),
            pltpu.SemaphoreType.DMA((2, 2)),
        ],
        compiler_params=params(),
        cost_estimate=brief(),
        name="feed_forward",
    )(late, gain_row, cotangent, w_gu, w_down)
    if not packed:
        down = pack_down(grads[1].reshape(count, extent, D), shard_rows).reshape(D, -1)
        grads = [jnp.concatenate([grads[0], down], axis=1)]
    return result, grad, gain_grad, grads[0]


def grad_kernel(spans, count, core_ref, *refs):
    groups = len(spans)
    sides, (keep_ref, send_ref, flipped_ref) = refs[: 2 * groups], refs[2 * groups :]
    step = pl.program_id(0)
    even = core_ref[0] == 0
    rows = D // count
    for at, (begin, end) in enumerate(spans):
        left_ref, right_ref = sides[2 * at : 2 * at + 2]

        @pl.when(step == begin)
        def _(left_ref=left_ref):
            for start in range(0, left_ref.shape[0], 256):
                piece = slice(start, start + 256)
                flipped_ref[:, piece] = jnp.transpose(left_ref[piece, :])

        @pl.when((step >= begin) & (step < end))
        def _(right_ref=right_ref):
            product = matmul(flipped_ref[...], right_ref[...])
            view = product.reshape(count // 2, 2, rows, D)
            low = view[:, 0].reshape(D // 2, D).astype(BF16)
            high = view[:, 1].reshape(D // 2, D).astype(BF16)

            @pl.when(even)
            def _():
                keep_ref[...] = low
                send_ref[...] = high

            @pl.when(jnp.logical_not(even))
            def _():
                keep_ref[...] = high
                send_ref[...] = low


def weight_grads(pairs, count):
    rows = D // count
    if rows % 8:
        whole = jnp.concatenate([matmul_tn(*pair).astype(BF16) for pair in pairs], axis=1)
        view = whole.reshape(count // 2, 2, rows, -1)
        mine = my_bit(1)
        return [
            lax.dynamic_index_in_dim(view, bit, 1, False).reshape(D // 2, -1)
            for bit in (mine, 1 - mine)
        ]
    spans = []
    in_specs = [pl.BlockSpec(memory_space=pltpu.SMEM)]
    total = 0
    for left, right in pairs:
        steps = right.shape[1] // D
        begin, end = total, total + steps
        spans.append((begin, end))
        in_specs.append(pl.BlockSpec(left.shape, lambda c: (0, 0)))
        in_specs.append(
            pl.BlockSpec(
                (right.shape[0], D),
                lambda c, begin=begin, end=end: (0, jnp.clip(c - begin, 0, end - begin - 1)),
            )
        )
        total = end
    tokens = pairs[0][0].shape[0]
    core = (lax.axis_index("fsdp") % 2).astype(jnp.int32).reshape(1)
    half = jax.ShapeDtypeStruct((D // 2, total * D), BF16)
    return pl.pallas_call(
        partial(grad_kernel, tuple(spans), count),
        grid=(total,),
        in_specs=in_specs,
        out_specs=[pl.BlockSpec((D // 2, D), lambda c: (0, c))] * 2,
        out_shape=[half, half],
        scratch_shapes=[pltpu.VMEM((D, tokens), BF16)],
        compiler_params=params(),
        cost_estimate=brief(),
        name="weight_grads",
    )(core, *[side for pair in pairs for side in pair])


DOWN_BLOCKS = -(-FF // D)
FEED_STAGE = 3
SELF_WIDTHS = (3 * INNER, D)
CROSS_WIDTHS = (INNER, 2 * INNER, D)
MIDDLE_WIDTHS = CROSS_WIDTHS + (D,)
FEED_WIDTHS = (2 * FF, DOWN_BLOCKS * D)


def interleave(parts, unit):
    pieces = []
    for start in range(0, parts[0].shape[1], unit):
        pieces.extend(part[:, start : start + unit] for part in parts)
    return pieces


def deinterleave(block, count, unit):
    stride = count * unit
    return [
        jnp.concatenate(
            [block[:, s + at * unit : s + (at + 1) * unit] for s in range(0, block.shape[1], stride)],
            axis=1,
        )
        for at in range(count)
    ]


def row_blocks(flat_parts, width):
    joined = jnp.concatenate(flat_parts).reshape(-1, width)
    each = flat_parts[0].shape[0] // width
    return [joined[at * each : (at + 1) * each] for at in range(len(flat_parts))]


def flat_blocks(blocks):
    each = blocks[0].shape[0] * blocks[0].shape[1]
    joined = jnp.concatenate(blocks, axis=0).reshape(-1)
    return [joined[at * each : (at + 1) * each] for at in range(len(blocks))]


def pack_down(stacked, rows):
    pieces = [stacked[:, at * rows : (at + 1) * rows] for at in range(DOWN_BLOCKS)]
    lack = rows - pieces[-1].shape[1]
    pieces[-1] = jnp.pad(pieces[-1], ((0, 0), (0, lack), (0, 0)))
    return jnp.concatenate(pieces, axis=2)


def unpack_down(stacked, extent):
    rows = stacked.shape[1]
    pieces = []
    for at in range(DOWN_BLOCKS):
        kept = min(rows, extent - at * rows)
        pieces.append(stacked[:, :kept, at * D : (at + 1) * D])
    return jnp.concatenate(pieces, axis=1)


def swap(values, bit, count):
    return lax.ppermute(values, "fsdp", [(index, index ^ bit) for index in range(count)])


def bit_orders(count):
    bits = []
    bit = count // 2
    while bit > 1:
        bits.append(bit)
        bit //= 2
    other = bits[:-2] + bits[-2:][::-1]
    return (tuple(bits) + (1,), tuple(other) + (1,))


def my_bit(bit):
    return (lax.axis_index("fsdp") // bit) % 2


def gather_rows(shard, filler, count):
    width = shard.shape[1] // 2
    orders = bit_orders(count)
    parts = [shard[:, at * width : (at + 1) * width] for at in range(2)]
    known = [[], []]
    for stage in range(len(orders[0])):
        for at in range(2):
            bit = orders[at][stage]
            place = sum(1 for other in known[at] if other > bit)
            theirs = swap(parts[at], bit, count)
            if stage == 1 and at == 1:
                theirs, filler = lax.optimization_barrier((theirs, filler))
            mine = parts[at]
            first = my_bit(bit) == 0
            parts[at] = jnp.stack(
                [jnp.where(first, mine, theirs), jnp.where(first, theirs, mine)], axis=place
            )
            known[at].append(bit)
    return (jnp.concatenate([part.reshape(-1, width) for part in parts], axis=1), filler)


def scatter_rows(keep, send, count):
    rows = D // count
    width = keep.shape[1] // 2
    (got,) = yield [swap(send, 1, count)]
    total = (keep.astype(F32) + got.astype(F32)).astype(BF16)
    parts = [total[:, at * width : (at + 1) * width] for at in range(2)]
    orders = [order[:-1][::-1] for order in bit_orders(count)]
    left = [sorted(order) for order in orders]
    last = len(orders[0]) - 1
    for stage in range(last + 1):
        kept = []
        gots = []
        for at in range(2):
            bit = orders[at][stage]
            inner = 2 ** left[at].index(bit)
            outer = 2 ** (len(left[at]) - 1) // inner
            view = parts[at].reshape(outer, 2, inner * rows, width)
            mine = my_bit(bit)
            kept.append(lax.dynamic_slice_in_dim(view, mine, 1, 1))
            gots.append(swap(lax.dynamic_slice_in_dim(view, 1 - mine, 1, 1), bit, count))
            left[at].remove(bit)
        gots = yield gots
        for at in range(2):
            total = kept[at].astype(F32) + gots[at].astype(F32)
            parts[at] = (total if stage == last else total.astype(BF16)).reshape(-1, width)
    return jnp.concatenate(parts, axis=1)


def tie(*values):
    return lax.optimization_barrier(values)


def step(transfer, gots):
    try:
        return (transfer.send(gots), None)
    except StopIteration as end:
        return (None, end.value)


def finish(transfer, gots):
    result = None
    while gots is not None:
        gots, result = step(transfer, gots)
    return result


def sum_everywhere(values, count):
    bits = []
    bit = 1
    while bit < count:
        bits.append(bit)
        bit *= 2
    for bit in bits[:-2]:
        (got,) = yield [swap(values, bit, count)]
        values = values + got
    one, two = bits[-2:]
    near, far, both = yield [swap(values, hop, count) for hop in (one, two, one + two)]
    return (values + near) + (far + both)


def cut(block, widths):
    pieces = []
    start = 0
    for width in widths:
        pieces.append(block[:, start : start + width])
        start += width
    return pieces


def per_device(
    count,
    tokens,
    encoder_states,
    self_query,
    self_key,
    self_value,
    self_out,
    cross_query,
    cross_key,
    cross_value,
    cross_out,
    ff_gate,
    ff_up,
    ff_down,
    norm_gains,
    bias_table,
    buckets,
    cotangent,
):
    shards = (
        self_query,
        self_key,
        self_value,
        self_out,
        cross_query,
        cross_key,
        cross_value,
        cross_out,
        ff_gate,
        ff_up,
        ff_down,
    )
    r_sq, r_sk, r_sv, r_so, r_cq, r_ck, r_cv, r_co = row_blocks(shards[:8], D)
    r_gate, r_up = row_blocks(shards[8:10], FF)
    rows = r_sq.shape[0]
    self_shard = jnp.concatenate(interleave([r_sq, r_sk, r_sv], WIDE) + [r_so], axis=1)
    cross_shard = [r_cq] + interleave([r_ck, r_cv], WIDE) + [r_co]
    down_shard = pack_down(shards[10].reshape(1, -1, D), rows)[0]
    rest_shard = jnp.concatenate(
        interleave([r_gate, r_up], CHUNK) + [down_shard] + cross_shard, axis=1
    )
    rest = lax.all_gather(rest_shard, "fsdp", axis=0, tiled=True)
    _, w_down, w_cq, w_ckv, w_co = cut(rest, FEED_WIDTHS + CROSS_WIDTHS)
    w_down = unpack_down(w_down.reshape(count, rows, -1), FF // count).reshape(FF, D)

    gain_values = norm_gains.astype(F32)
    length = buckets.shape[0]
    bucket_of = buckets[:, 0]
    onehot = (bucket_of[None, :] == jnp.arange(BUCKETS, dtype=jnp.int32)[:, None]).astype(F32)
    distance_bias = jnp.take(bias_table, bucket_of, axis=0).T
    bias = expand_bias(distance_bias, length)

    inputs = tokens.astype(F32)
    factor_one = norm_factor(inputs)
    normed_one = (inputs * factor_one * gain_values[0]).astype(BF16)
    self_weights, (bias, normed_one) = gather_rows(self_shard, (bias, normed_one), count)
    w_qkv, w_so = cut(self_weights, SELF_WIDTHS)
    qkv = matmul(normed_one, w_qkv).astype(BF16)
    kv_two = matmul(encoder_states, w_ckv).astype(BF16)
    mixed_one, log_one = self_forward(qkv, bias, length)
    middle = inputs + matmul(mixed_one, w_so)
    factor_two = norm_factor(middle)
    normed_two = (middle * factor_two * gain_values[1]).astype(BF16)
    query_two = matmul(normed_two, w_cq).astype(BF16)
    mixed_two, log_two = cross_forward(query_two, kv_two, length)
    late = middle + matmul(mixed_two, w_co)
    result_rows, late_grad, gain_three, feed_packed = feed_forward(
        late, gain_values[2:3], cotangent, rest, w_down, count
    )
    late_grad, feed_packed = lax.optimization_barrier((late_grad, feed_packed))
    feed_owned = lax.psum_scatter(feed_packed, "fsdp", scatter_dimension=0, tiled=True)
    late_branch = late_grad.astype(BF16)
    mixed_grad = matmul_nt(late_branch, w_co).astype(BF16)
    query_grad, kv_grad = cross_backward(query_two, kv_two, mixed_grad, log_two, length)
    norm_grad, gain_two = norm_backward(
        middle, factor_two, gain_values[1], matmul_nt(query_grad, w_cq)
    )
    middle_grad = late_grad + norm_grad
    branch_grad = middle_grad.astype(BF16)
    keep, send = weight_grads(
        [
            (normed_two, query_grad),
            (encoder_states, kv_grad),
            (mixed_two, late_branch),
            (mixed_one, branch_grad),
        ],
        count,
    )
    mixed_grad = matmul_nt(branch_grad, w_so).astype(BF16)
    encoder_grad = matmul_nt(kv_grad, w_ckv).astype(BF16)
    middle_transfer = scatter_rows(keep, send, count)
    middle_gots = next(middle_transfer)
    middle_gots, mixed_grad, encoder_grad = tie(middle_gots, mixed_grad, encoder_grad)
    middle_gots = middle_transfer.send(middle_gots)
    qkv_grad, sheared = self_backward(qkv, mixed_grad, log_one, bias, length)
    middle_gots, qkv_grad, sheared = tie(middle_gots, qkv_grad, sheared)
    middle_gots = middle_transfer.send(middle_gots)
    keep, send = weight_grads([(normed_one, qkv_grad)], count)
    middle_gots, keep, send, qkv_grad = tie(middle_gots, keep, send, qkv_grad)
    middle_gots = middle_transfer.send(middle_gots)
    last_transfer = scatter_rows(keep, send, count)
    last_gots = next(last_transfer)
    norm_grad, gain_one = norm_backward(
        inputs, factor_one, gain_values[0], matmul_nt(qkv_grad, w_qkv)
    )
    input_grad = (middle_grad + norm_grad).astype(BF16)
    middle_gots, last_gots, input_grad, gain_one = tie(middle_gots, last_gots, input_grad, gain_one)
    last_gots = last_transfer.send(last_gots)
    middle_owned = finish(middle_transfer, middle_gots)
    by_distance = sum(
        jnp.pad(sheared[:, row, row:], ((0, 0), (0, row))) for row in range(sheared.shape[1])
    )
    table_part = jnp.sum(onehot[:, None, :] * by_distance[None, :, :], axis=-1)
    gains_part = jnp.stack([gain_one, gain_two, gain_three[0]])
    small = jnp.concatenate([gains_part.reshape(-1), table_part.reshape(-1)]).reshape(-1, 128)
    small_transfer = sum_everywhere(small, count)
    small_gots = next(small_transfer)
    stage = 1
    while last_gots is not None:
        if small_gots is not None:
            last_gots, small_gots = tie(last_gots, small_gots)
            small_gots, small = step(small_transfer, small_gots)
        if stage == FEED_STAGE:
            last_gots, feed_owned = tie(last_gots, feed_owned)
        last_gots, self_owned = step(last_transfer, last_gots)
        stage += 1
    if small_gots is not None:
        small = finish(small_transfer, small_gots)
    small = small.reshape(-1)
    o_gu, o_down = cut(feed_owned.astype(F32), FEED_WIDTHS)

    o_cq, o_ckv, o_co, o_so = cut(middle_owned, MIDDLE_WIDTHS)
    g_sq, g_sk, g_sv = flat_blocks(deinterleave(self_owned, 3, WIDE))
    g_cq, g_ck, g_cv, g_co, g_so = flat_blocks([o_cq] + deinterleave(o_ckv, 2, WIDE) + [o_co, o_so])
    g_gate, g_up = flat_blocks(deinterleave(o_gu, 2, CHUNK))
    g_down = unpack_down(o_down[None], FF // count)[0].reshape(-1)

    gains_grad = small[: 3 * D].reshape(3, D)
    table_grad = small[3 * D :].reshape(BUCKETS, HEADS)
    return (
        result_rows,
        input_grad,
        encoder_grad,
        g_sq,
        g_sk,
        g_sv,
        g_so,
        g_cq,
        g_ck,
        g_cv,
        g_co,
        g_gate,
        g_up,
        g_down,
        gains_grad,
        table_grad,
    )


def solution(mesh):
    flat = P("fsdp")
    rows = P("fsdp", None)
    return jax.shard_map(
        partial(per_device, mesh.shape["fsdp"]),
        mesh=mesh,
        in_specs=(rows, rows) + (flat,) * 11 + (P(), P(), P(), rows),
        out_specs=(rows, rows, rows) + (flat,) * 11 + (P(), P()),
        check_vma=False,
    )
```

```python
from functools import partial

import jax
import jax.numpy as jnp
from jax import lax
from jax.experimental import pallas as pl
from jax.experimental.pallas import tpu as pltpu
from jax.sharding import PartitionSpec as P

D = 768
HEADS = 12
HD = 64
FF = 2048
BUCKETS = 32
INNER = 768
PAIRS = HEADS // 2
WIDE = 2 * HD

EPSILON = 1e-06
NEGATIVE = -1e30
VMEM_LIMIT = 48 * 1024 * 1024
F32 = jnp.float32
BF16 = jnp.bfloat16


def params():
    return pltpu.CompilerParams(vmem_limit_bytes=VMEM_LIMIT)


def brief():
    return pl.CostEstimate(flops=1_000_000, bytes_accessed=100_000, transcendentals=0)


def matmul(left_side, right_side):
    return jnp.dot(left_side, right_side, preferred_element_type=F32)


def matmul_tn(left_side, right_side):
    return lax.dot_general(
        left_side, right_side, (((0,), (0,)), ((), ())), preferred_element_type=F32
    )


def matmul_nt(left_side, right_side):
    return lax.dot_general(
        left_side, right_side, (((1,), (1,)), ((), ())), preferred_element_type=F32
    )


def norm_factor(inputs):
    return lax.rsqrt(jnp.mean(inputs * inputs, axis=-1, keepdims=True) + EPSILON)


def norm_backward(inputs, factor, gain_row, upstream):
    scaled = gain_row * upstream
    inner_mean = jnp.mean(scaled * inputs, axis=-1, keepdims=True)
    input_grad = factor * (scaled - inputs * factor * factor * inner_mean)
    return (input_grad, jnp.sum(upstream * inputs * factor, axis=0))


BAND = 16


def bias_kernel(band_ref, out_ref):
    length = out_ref.shape[1]
    band = band_ref[0]
    for group in range(length // BAND):
        rolled = pltpu.roll(band, length + BAND * group, 1)
        out_ref[0, group * BAND : (group + 1) * BAND, :] = rolled[:, :length].astype(BF16)


def expand_bias(distance_bias, length):
    extended = jnp.concatenate(
        [jnp.full((HEADS, length), NEGATIVE, F32), distance_bias.astype(F32)], axis=1
    )
    rows = [
        jnp.pad(extended[:, : 2 * length - row], ((0, 0), (row, 0)), constant_values=NEGATIVE)
        for row in range(BAND)
    ]
    bands = jnp.stack(rows, axis=1)
    return pl.pallas_call(
        bias_kernel,
        grid=(HEADS,),
        in_specs=[pl.BlockSpec((1, BAND, 2 * length), lambda h: (h, 0, 0))],
        out_specs=pl.BlockSpec((1, length, length), lambda h: (h, 0, 0)),
        out_shape=jax.ShapeDtypeStruct((HEADS, length, length), BF16),
        compiler_params=params(),
        name="bias",
    )(bands)


def head_masks():
    lanes = lax.broadcasted_iota(jnp.int32, (1, WIDE), 1)
    low = (lanes < HD).astype(F32).astype(BF16)
    high = (lanes >= HD).astype(F32).astype(BF16)
    return (low, high)


def attend_core(queries, keys, values, bias_ref, out_ref, log_ref):
    length = queries.shape[0]
    causal = bias_ref is not None
    masks = head_masks()
    step = length // 2
    for part in range(2):
        begin, end = part * step, (part + 1) * step
        reach = end if causal else keys.shape[0]
        mixed = None
        for head in range(2):
            scores = matmul_nt(keys[:reach] * masks[head], queries[begin:end])
            if causal:
                scores = scores + bias_ref[head, :reach, begin:end].astype(F32)
            top = jnp.max(scores, axis=0, keepdims=True)
            powered = jnp.exp(scores - top)
            total = jnp.sum(powered, axis=0, keepdims=True)
            probs = (powered * (1.0 / total)).astype(BF16)
            term = matmul_tn(values[:reach] * masks[head], probs)
            mixed = term if mixed is None else mixed + term
            log_ref[0, 0, head : head + 1, begin:end] = top + jnp.log(total)
        out_ref[begin:end, :] = jnp.transpose(mixed).astype(BF16)


def self_forward_kernel(qkv_ref, bias_ref, out_ref, log_ref):
    attend_core(
        qkv_ref[:, :WIDE],
        qkv_ref[:, WIDE : 2 * WIDE],
        qkv_ref[:, 2 * WIDE :],
        bias_ref,
        out_ref,
        log_ref,
    )


def cross_forward_kernel(q_ref, kv_ref, out_ref, log_ref):
    attend_core(q_ref[...], kv_ref[:, :WIDE], kv_ref[:, WIDE:], None, out_ref, log_ref)


def self_forward(qkv, bias, length):
    seqs = qkv.shape[0] // length
    return pl.pallas_call(
        self_forward_kernel,
        grid=(PAIRS, seqs),
        in_specs=[
            pl.BlockSpec((length, 3 * WIDE), lambda p, s: (s, p)),
            pl.BlockSpec((2, length, length), lambda p, s: (p, 0, 0)),
        ],
        out_specs=[
            pl.BlockSpec((length, WIDE), lambda p, s: (s, p)),
            pl.BlockSpec((1, 1, 2, length), lambda p, s: (s, p, 0, 0)),
        ],
        out_shape=[
            jax.ShapeDtypeStruct((qkv.shape[0], INNER), BF16),
            jax.ShapeDtypeStruct((seqs, PAIRS, 2, length), F32),
        ],
        compiler_params=params(),
        cost_estimate=brief(),
        name="self_forward",
    )(qkv, bias)


def cross_forward(queries, kv, length):
    seqs = queries.shape[0] // length
    extent = kv.shape[0] // seqs
    return pl.pallas_call(
        cross_forward_kernel,
        grid=(PAIRS, seqs),
        in_specs=[
            pl.BlockSpec((length, WIDE), lambda p, s: (s, p)),
            pl.BlockSpec((extent, 2 * WIDE), lambda p, s: (s, p)),
        ],
        out_specs=[
            pl.BlockSpec((length, WIDE), lambda p, s: (s, p)),
            pl.BlockSpec((1, 1, 2, length), lambda p, s: (s, p, 0, 0)),
        ],
        out_shape=[
            jax.ShapeDtypeStruct((queries.shape[0], INNER), BF16),
            jax.ShapeDtypeStruct((seqs, PAIRS, 2, length), F32),
        ],
        compiler_params=params(),
        cost_estimate=brief(),
        name="cross_forward",
    )(queries, kv)


def attend_back_core(queries, keys, values, upstream, log_ref, bias_ref, store_q, store_kv, table):
    length = queries.shape[0]
    causal = bias_ref is not None
    masks = head_masks()
    step = length // 2
    key_grad = [None, None]
    value_grad = [None, None]

    def put(parts, at, term):
        parts[at] = term if parts[at] is None else parts[at] + term

    half = keys.shape[0] // 2
    for part in range(2):
        begin, end = part * step, (part + 1) * step
        reach = end if causal else keys.shape[0]
        query_grad = None
        for head in range(2):
            mask = masks[head]
            masked_keys = keys[:reach] * mask
            masked_query = queries[begin:end] * mask
            masked_up = upstream[begin:end] * mask
            scores = matmul_nt(masked_keys, queries[begin:end])
            if causal:
                scores = scores + bias_ref[head, :reach, begin:end].astype(F32)
            probs = jnp.exp(scores - log_ref[0, 0, head : head + 1, begin:end])
            prob_grad = matmul_nt(values[:reach], masked_up)
            delta = jnp.sum(probs * prob_grad, axis=0, keepdims=True)
            score_grad = probs * (prob_grad - delta)
            if table is not None:
                table(head, begin, end, reach, score_grad)
            low_grad = score_grad.astype(BF16)
            low_probs = probs.astype(BF16)
            for block in range(reach // half):
                rows = slice(block * half, (block + 1) * half)
                put(value_grad, block, matmul(low_probs[rows], masked_up))
                put(key_grad, block, matmul(low_grad[rows], masked_query))
            term = matmul_tn(masked_keys, low_grad)
            query_grad = term if query_grad is None else query_grad + term
        store_q(begin, end, jnp.transpose(query_grad).astype(BF16))
    for block in range(2):
        store_kv(
            block * half, (block + 1) * half, key_grad[block].astype(BF16), value_grad[block].astype(BF16)
        )


SHEAR = 128


def self_backward_kernel(qkv_ref, up_ref, log_ref, bias_ref, grad_ref, table_ref, shear_ref):
    length = qkv_ref.shape[0]

    @pl.when(pl.program_id(1) == 0)
    def _():
        shear_ref[...] = jnp.zeros_like(shear_ref)

    def table(head, begin, end, reach, score_grad):
        for block in range(reach // SHEAR):
            start = max(begin, block * SHEAR)
            shear_ref[head, :, start - block * SHEAR : end - block * SHEAR] += score_grad[
                block * SHEAR : (block + 1) * SHEAR, start - begin : end - begin
            ]

    def store_q(begin, end, grad):
        grad_ref[begin:end, :WIDE] = grad

    def store_kv(begin, end, key_grad, value_grad):
        grad_ref[begin:end, WIDE : 2 * WIDE] = key_grad
        grad_ref[begin:end, 2 * WIDE :] = value_grad

    attend_back_core(
        qkv_ref[:, :WIDE],
        qkv_ref[:, WIDE : 2 * WIDE],
        qkv_ref[:, 2 * WIDE :],
        up_ref[...],
        log_ref,
        bias_ref,
        store_q,
        store_kv,
        table,
    )

    @pl.when(pl.program_id(1) == pl.num_programs(1) - 1)
    def _():
        for head in range(2):
            total = shear_ref[head, 0:8, :]
            for group in range(1, SHEAR // 8):
                rows = shear_ref[head, 8 * group : 8 * group + 8, :]
                total = total + pltpu.roll(rows, length - 8 * group, 1)
            table_ref[head] = total


def cross_backward_kernel(q_ref, kv_ref, up_ref, log_ref, dq_ref, dkv_ref):
    def store_q(begin, end, grad):
        dq_ref[begin:end, :] = grad

    def store_kv(begin, end, key_grad, value_grad):
        dkv_ref[begin:end, :WIDE] = key_grad
        dkv_ref[begin:end, WIDE:] = value_grad

    attend_back_core(
        q_ref[...],
        kv_ref[:, :WIDE],
        kv_ref[:, WIDE:],
        up_ref[...],
        log_ref,
        None,
        store_q,
        store_kv,
        None,
    )


def self_backward(qkv, upstream, logs, bias, length):
    seqs = qkv.shape[0] // length
    return pl.pallas_call(
        self_backward_kernel,
        grid=(PAIRS, seqs),
        in_specs=[
            pl.BlockSpec((length, 3 * WIDE), lambda p, s: (s, p)),
            pl.BlockSpec((length, WIDE), lambda p, s: (s, p)),
            pl.BlockSpec((1, 1, 2, length), lambda p, s: (s, p, 0, 0)),
            pl.BlockSpec((2, length, length), lambda p, s: (p, 0, 0)),
        ],
        out_specs=[
            pl.BlockSpec((length, 3 * WIDE), lambda p, s: (s, p)),
            pl.BlockSpec((2, 8, length), lambda p, s: (p, 0, 0)),
        ],
        out_shape=[
            jax.ShapeDtypeStruct(qkv.shape, BF16),
            jax.ShapeDtypeStruct((HEADS, 8, length), F32),
        ],
        scratch_shapes=[pltpu.VMEM((2, SHEAR, length), F32)],
        compiler_params=params(),
        cost_estimate=brief(),
        name="self_backward",
    )(qkv, upstream, logs, bias)


def cross_backward(queries, kv, upstream, logs, length):
    seqs = queries.shape[0] // length
    extent = kv.shape[0] // seqs
    return pl.pallas_call(
        cross_backward_kernel,
        grid=(PAIRS, seqs),
        in_specs=[
            pl.BlockSpec((length, WIDE), lambda p, s: (s, p)),
            pl.BlockSpec((extent, 2 * WIDE), lambda p, s: (s, p)),
            pl.BlockSpec((length, WIDE), lambda p, s: (s, p)),
            pl.BlockSpec((1, 1, 2, length), lambda p, s: (s, p, 0, 0)),
        ],
        out_specs=[
            pl.BlockSpec((length, WIDE), lambda p, s: (s, p)),
            pl.BlockSpec((extent, 2 * WIDE), lambda p, s: (s, p)),
        ],
        out_shape=[
            jax.ShapeDtypeStruct(queries.shape, BF16),
            jax.ShapeDtypeStruct(kv.shape, BF16),
        ],
        compiler_params=params(),
        cost_estimate=brief(),
        name="cross_backward",
    )(queries, kv, upstream, logs)


CHUNK = 256
ROOT = 0.7978845608028654
CUBIC = 0.044715


def feed_kernel(
    extent,
    packed,
    late_ref,
    gain_ref,
    up_ref,
    wgu_ref,
    wd_ref,
    *refs,
):
    result_ref, grad_ref, gain_grad_ref, ggu_out = refs[:4]
    gd_out = ggu_out if packed else refs[4]
    normed_ref, flipped_ref, total_ref, hidden_ref, dgu_ref, ggu_buf, gd_buf, sems = refs[-8:]
    step = pl.program_id(0)
    slot = lax.rem(step, 2)
    rows = late_ref.shape[0]
    block = min(rows, 256)

    def copies(at, place):
        columns = pl.ds(pl.multiple_of(at * 2 * CHUNK, 2 * CHUNK), 2 * CHUNK)
        height = gd_buf.shape[1]
        down_rows = pl.ds(pl.multiple_of(at * height, 32), height)
        side = pl.ds(2 * FF, DOWN_BLOCKS * D) if packed else pl.ds(0, D)
        return (
            pltpu.make_async_copy(ggu_buf.at[place], ggu_out.at[:, columns], sems.at[place, 0]),
            pltpu.make_async_copy(gd_buf.at[place], gd_out.at[down_rows, side], sems.at[place, 1]),
        )

    @pl.when(step >= 2)
    def _():
        for copy in copies(step - 2, slot):
            copy.wait()

    @pl.when(step == 0)
    def _():
        for begin in range(0, rows, block):
            piece = slice(begin, begin + block)
            late = late_ref[piece, :]
            normed = (late * norm_factor(late) * gain_ref[...]).astype(BF16)
            normed_ref[piece, :] = normed
            flipped_ref[:, piece] = jnp.transpose(normed)
        total_ref[...] = late_ref[...]
        grad_ref[...] = jnp.zeros_like(grad_ref)

    for begin in range(0, rows, block):
        piece = slice(begin, begin + block)
        both = matmul(normed_ref[piece, :], wgu_ref[...])
        gate = both[:, :CHUNK]
        up = both[:, CHUNK:]
        hidden_grad = matmul_nt(up_ref[piece, :], wd_ref[...])
        square = gate * gate
        bent = jnp.tanh(ROOT * gate * (1.0 + CUBIC * square))
        half = 0.5 + 0.5 * bent
        activated = gate * half
        slope = half + 0.5 * gate * (1.0 - bent * bent) * (ROOT + (3.0 * ROOT * CUBIC) * square)
        hidden = (activated * up).astype(BF16)
        hidden_ref[piece, :] = hidden
        dgu_ref[piece, :CHUNK] = (hidden_grad * up * slope).astype(BF16)
        dgu_ref[piece, CHUNK:] = (hidden_grad * activated).astype(BF16)
        total_ref[piece, :] += matmul(hidden, wd_ref[...])
        grad_ref[piece, :] += matmul_nt(dgu_ref[piece, :], wgu_ref[...])
    ggu_buf[slot] = matmul(flipped_ref[...], dgu_ref[...]).astype(BF16)
    down_grad = matmul_tn(hidden_ref[...], up_ref[...])
    if packed:
        owners = CHUNK // extent
        shard_rows = gd_buf.shape[1] // owners
        view = down_grad.reshape(owners, extent, D)
        for at in range(DOWN_BLOCKS):
            piece = view[:, at * shard_rows : (at + 1) * shard_rows]
            lack = shard_rows - piece.shape[1]
            if lack:
                piece = jnp.concatenate([piece, jnp.zeros((owners, lack, D), F32)], axis=1)
            piece = piece.reshape(owners * shard_rows, D)
            gd_buf[slot, :, at * D : (at + 1) * D] = piece.astype(BF16)
    else:
        gd_buf[slot] = down_grad.astype(BF16)
    for copy in copies(step, slot):
        copy.start()

    @pl.when(step == pl.num_programs(0) - 1)
    def _():
        gain_grad = None
        for begin in range(0, rows, block):
            piece = slice(begin, begin + block)
            late = late_ref[piece, :]
            result_ref[piece, :] = total_ref[piece, :].astype(BF16)
            norm_grad, gain_part = norm_backward(
                late, norm_factor(late), gain_ref[...], grad_ref[piece, :]
            )
            grad_ref[piece, :] = up_ref[piece, :].astype(F32) + norm_grad
            gain_grad = gain_part if gain_grad is None else gain_grad + gain_part
        gain_grad_ref[...] = gain_grad[None, :]
        for copy in copies(step - 1, 1 - slot) + copies(step, slot):
            copy.wait()


def feed_forward(late, gain_row, cotangent, w_gu, w_down, count):
    rows = late.shape[0]
    whole = lambda c: (0, 0)
    extent = FF // count
    shard_rows = D // count
    packed = shard_rows % 8 == 0 and extent % 8 == 0 and CHUNK % extent == 0
    packed = packed and CHUNK // extent * shard_rows % 32 == 0
    if packed:
        down_block = (CHUNK // extent * shard_rows, DOWN_BLOCKS * D)
        grads = [jax.ShapeDtypeStruct((D, 2 * FF + DOWN_BLOCKS * D), BF16)]
    else:
        down_block = (CHUNK, D)
        grads = [jax.ShapeDtypeStruct((D, 2 * FF), BF16), jax.ShapeDtypeStruct((FF, D), BF16)]
    result, grad, gain_grad, *grads = pl.pallas_call(
        partial(feed_kernel, extent, packed),
        grid=(FF // CHUNK,),
        in_specs=[
            pl.BlockSpec((rows, D), whole),
            pl.BlockSpec((1, D), whole),
            pl.BlockSpec((rows, D), whole),
            pl.BlockSpec((D, 2 * CHUNK), lambda c: (0, c)),
            pl.BlockSpec((CHUNK, D), lambda c: (c, 0)),
        ],
        out_specs=[
            pl.BlockSpec((rows, D), whole),
            pl.BlockSpec((rows, D), whole),
            pl.BlockSpec((1, D), whole),
        ]
        + [pl.BlockSpec(memory_space=pl.ANY)] * len(grads),
        out_shape=[
            jax.ShapeDtypeStruct((rows, D), BF16),
            jax.ShapeDtypeStruct((rows, D), F32),
            jax.ShapeDtypeStruct((1, D), F32),
        ]
        + grads,
        scratch_shapes=[
            pltpu.VMEM((rows, D), BF16),
            pltpu.VMEM((D, rows), BF16),
            pltpu.VMEM((rows, D), F32),
            pltpu.VMEM((rows, CHUNK), BF16),
            pltpu.VMEM((rows, 2 * CHUNK), BF16),
            pltpu.VMEM((2, D, 2 * CHUNK), BF16),
            pltpu.VMEM((2,) + down_block, BF16),
            pltpu.SemaphoreType.DMA((2, 2)),
        ],
        compiler_params=params(),
        cost_estimate=brief(),
        name="feed_forward",
    )(late, gain_row, cotangent, w_gu, w_down)
    if not packed:
        down = pack_down(grads[1].reshape(count, extent, D), shard_rows).reshape(D, -1)
        grads = [jnp.concatenate([grads[0], down], axis=1)]
    return result, grad, gain_grad, grads[0]


def grad_kernel(spans, count, core_ref, *refs):
    groups = len(spans)
    sides, (keep_ref, send_ref, flipped_ref) = refs[: 2 * groups], refs[2 * groups :]
    step = pl.program_id(0)
    even = core_ref[0] == 0
    rows = D // count
    for at, (begin, end) in enumerate(spans):
        left_ref, right_ref = sides[2 * at : 2 * at + 2]

        @pl.when(step == begin)
        def _(left_ref=left_ref):
            for start in range(0, left_ref.shape[0], 256):
                piece = slice(start, start + 256)
                flipped_ref[:, piece] = jnp.transpose(left_ref[piece, :])

        @pl.when((step >= begin) & (step < end))
        def _(right_ref=right_ref):
            product = matmul(flipped_ref[...], right_ref[...])
            view = product.reshape(count // 2, 2, rows, D)
            low = view[:, 0].reshape(D // 2, D).astype(BF16)
            high = view[:, 1].reshape(D // 2, D).astype(BF16)

            @pl.when(even)
            def _():
                keep_ref[...] = low
                send_ref[...] = high

            @pl.when(jnp.logical_not(even))
            def _():
                keep_ref[...] = high
                send_ref[...] = low


def weight_grads(pairs, count):
    rows = D // count
    if rows % 8:
        whole = jnp.concatenate([matmul_tn(*pair).astype(BF16) for pair in pairs], axis=1)
        view = whole.reshape(count // 2, 2, rows, -1)
        mine = my_bit(1)
        return [
            lax.dynamic_index_in_dim(view, bit, 1, False).reshape(D // 2, -1)
            for bit in (mine, 1 - mine)
        ]
    spans = []
    in_specs = [pl.BlockSpec(memory_space=pltpu.SMEM)]
    total = 0
    for left, right in pairs:
        steps = right.shape[1] // D
        begin, end = total, total + steps
        spans.append((begin, end))
        in_specs.append(pl.BlockSpec(left.shape, lambda c: (0, 0)))
        in_specs.append(
            pl.BlockSpec(
                (right.shape[0], D),
                lambda c, begin=begin, end=end: (0, jnp.clip(c - begin, 0, end - begin - 1)),
            )
        )
        total = end
    tokens = pairs[0][0].shape[0]
    core = (lax.axis_index("fsdp") % 2).astype(jnp.int32).reshape(1)
    half = jax.ShapeDtypeStruct((D // 2, total * D), BF16)
    return pl.pallas_call(
        partial(grad_kernel, tuple(spans), count),
        grid=(total,),
        in_specs=in_specs,
        out_specs=[pl.BlockSpec((D // 2, D), lambda c: (0, c))] * 2,
        out_shape=[half, half],
        scratch_shapes=[pltpu.VMEM((D, tokens), BF16)],
        compiler_params=params(),
        cost_estimate=brief(),
        name="weight_grads",
    )(core, *[side for pair in pairs for side in pair])


DOWN_BLOCKS = -(-FF // D)
SELF_WIDTHS = (3 * INNER, D)
CROSS_WIDTHS = (INNER, 2 * INNER, D)
MIDDLE_WIDTHS = CROSS_WIDTHS + (D,)
FEED_WIDTHS = (2 * FF, DOWN_BLOCKS * D)


def interleave(parts, unit):
    pieces = []
    for start in range(0, parts[0].shape[1], unit):
        pieces.extend(part[:, start : start + unit] for part in parts)
    return pieces


def deinterleave(block, count, unit):
    stride = count * unit
    return [
        jnp.concatenate(
            [block[:, s + at * unit : s + (at + 1) * unit] for s in range(0, block.shape[1], stride)],
            axis=1,
        )
        for at in range(count)
    ]


def row_blocks(flat_parts, width):
    joined = jnp.concatenate(flat_parts).reshape(-1, width)
    each = flat_parts[0].shape[0] // width
    return [joined[at * each : (at + 1) * each] for at in range(len(flat_parts))]


def flat_blocks(blocks):
    each = blocks[0].shape[0] * blocks[0].shape[1]
    joined = jnp.concatenate(blocks, axis=0).reshape(-1)
    return [joined[at * each : (at + 1) * each] for at in range(len(blocks))]


def pack_down(stacked, rows):
    pieces = [stacked[:, at * rows : (at + 1) * rows] for at in range(DOWN_BLOCKS)]
    lack = rows - pieces[-1].shape[1]
    pieces[-1] = jnp.pad(pieces[-1], ((0, 0), (0, lack), (0, 0)))
    return jnp.concatenate(pieces, axis=2)


def unpack_down(stacked, extent):
    rows = stacked.shape[1]
    pieces = []
    for at in range(DOWN_BLOCKS):
        kept = min(rows, extent - at * rows)
        pieces.append(stacked[:, :kept, at * D : (at + 1) * D])
    return jnp.concatenate(pieces, axis=1)


def swap(values, bit, count):
    return lax.ppermute(values, "fsdp", [(index, index ^ bit) for index in range(count)])


def bit_orders(count):
    bits = []
    bit = count // 2
    while bit > 1:
        bits.append(bit)
        bit //= 2
    other = bits[:-2] + bits[-2:][::-1]
    return (tuple(bits) + (1,), tuple(other) + (1,))


def my_bit(bit):
    return (lax.axis_index("fsdp") // bit) % 2


def gather_rows(shard, filler, count):
    width = shard.shape[1] // 2
    orders = bit_orders(count)
    parts = [shard[:, at * width : (at + 1) * width] for at in range(2)]
    known = [[], []]
    for stage in range(len(orders[0])):
        for at in range(2):
            bit = orders[at][stage]
            place = sum(1 for other in known[at] if other > bit)
            theirs = swap(parts[at], bit, count)
            if stage == 1 and at == 1:
                theirs, filler = lax.optimization_barrier((theirs, filler))
            mine = parts[at]
            first = my_bit(bit) == 0
            parts[at] = jnp.stack(
                [jnp.where(first, mine, theirs), jnp.where(first, theirs, mine)], axis=place
            )
            known[at].append(bit)
    return (jnp.concatenate([part.reshape(-1, width) for part in parts], axis=1), filler)


def scatter_rows(keep, send, count):
    rows = D // count
    width = keep.shape[1] // 2
    (got,) = yield [swap(send, 1, count)]
    total = (keep.astype(F32) + got.astype(F32)).astype(BF16)
    parts = [total[:, at * width : (at + 1) * width] for at in range(2)]
    orders = [order[:-1][::-1] for order in bit_orders(count)]
    left = [sorted(order) for order in orders]
    last = len(orders[0]) - 1
    for stage in range(last + 1):
        kept = []
        gots = []
        for at in range(2):
            bit = orders[at][stage]
            inner = 2 ** left[at].index(bit)
            outer = 2 ** (len(left[at]) - 1) // inner
            view = parts[at].reshape(outer, 2, inner * rows, width)
            mine = my_bit(bit)
            kept.append(lax.dynamic_slice_in_dim(view, mine, 1, 1))
            gots.append(swap(lax.dynamic_slice_in_dim(view, 1 - mine, 1, 1), bit, count))
            left[at].remove(bit)
        gots = yield gots
        for at in range(2):
            total = kept[at].astype(F32) + gots[at].astype(F32)
            parts[at] = (total if stage == last else total.astype(BF16)).reshape(-1, width)
    return jnp.concatenate(parts, axis=1)


def tie(*values):
    return lax.optimization_barrier(values)


def step(transfer, gots):
    try:
        return (transfer.send(gots), None)
    except StopIteration as end:
        return (None, end.value)


def finish(transfer, gots):
    result = None
    while gots is not None:
        gots, result = step(transfer, gots)
    return result


def sum_everywhere(values, count):
    bits = []
    bit = 1
    while bit < count:
        bits.append(bit)
        bit *= 2
    for bit in bits[:-2]:
        (got,) = yield [swap(values, bit, count)]
        values = values + got
    one, two = bits[-2:]
    near, far, both = yield [swap(values, hop, count) for hop in (one, two, one + two)]
    return (values + near) + (far + both)


def cut(block, widths):
    pieces = []
    start = 0
    for width in widths:
        pieces.append(block[:, start : start + width])
        start += width
    return pieces


def per_device(
    count,
    tokens,
    encoder_states,
    self_query,
    self_key,
    self_value,
    self_out,
    cross_query,
    cross_key,
    cross_value,
    cross_out,
    ff_gate,
    ff_up,
    ff_down,
    norm_gains,
    bias_table,
    buckets,
    cotangent,
):
    shards = (
        self_query,
        self_key,
        self_value,
        self_out,
        cross_query,
        cross_key,
        cross_value,
        cross_out,
        ff_gate,
        ff_up,
        ff_down,
    )
    r_sq, r_sk, r_sv, r_so, r_cq, r_ck, r_cv, r_co = row_blocks(shards[:8], D)
    r_gate, r_up = row_blocks(shards[8:10], FF)
    rows = r_sq.shape[0]
    self_shard = jnp.concatenate(interleave([r_sq, r_sk, r_sv], WIDE) + [r_so], axis=1)
    cross_shard = [r_cq] + interleave([r_ck, r_cv], WIDE) + [r_co]
    down_shard = pack_down(shards[10].reshape(1, -1, D), rows)[0]
    rest_shard = jnp.concatenate(
        interleave([r_gate, r_up], CHUNK) + [down_shard] + cross_shard, axis=1
    )
    rest = lax.all_gather(rest_shard, "fsdp", axis=0, tiled=True)
    _, w_down, w_cq, w_ckv, w_co = cut(rest, FEED_WIDTHS + CROSS_WIDTHS)
    w_down = unpack_down(w_down.reshape(count, rows, -1), FF // count).reshape(FF, D)

    gain_values = norm_gains.astype(F32)
    length = buckets.shape[0]
    bucket_of = buckets[:, 0]
    onehot = (bucket_of[None, :] == jnp.arange(BUCKETS, dtype=jnp.int32)[:, None]).astype(F32)
    distance_bias = jnp.take(bias_table, bucket_of, axis=0).T
    bias = expand_bias(distance_bias, length)

    inputs = tokens.astype(F32)
    factor_one = norm_factor(inputs)
    normed_one = (inputs * factor_one * gain_values[0]).astype(BF16)
    self_weights, (bias, normed_one) = gather_rows(self_shard, (bias, normed_one), count)
    w_qkv, w_so = cut(self_weights, SELF_WIDTHS)
    qkv = matmul(normed_one, w_qkv).astype(BF16)
    kv_two = matmul(encoder_states, w_ckv).astype(BF16)
    mixed_one, log_one = self_forward(qkv, bias, length)
    middle = inputs + matmul(mixed_one, w_so)
    factor_two = norm_factor(middle)
    normed_two = (middle * factor_two * gain_values[1]).astype(BF16)
    query_two = matmul(normed_two, w_cq).astype(BF16)
    mixed_two, log_two = cross_forward(query_two, kv_two, length)
    late = middle + matmul(mixed_two, w_co)
    result_rows, late_grad, gain_three, feed_packed = feed_forward(
        late, gain_values[2:3], cotangent, rest, w_down, count
    )
    late_grad, feed_packed = lax.optimization_barrier((late_grad, feed_packed))
    feed_owned = lax.psum_scatter(feed_packed, "fsdp", scatter_dimension=0, tiled=True)
    late_branch = late_grad.astype(BF16)
    mixed_grad = matmul_nt(late_branch, w_co).astype(BF16)
    query_grad, kv_grad = cross_backward(query_two, kv_two, mixed_grad, log_two, length)
    norm_grad, gain_two = norm_backward(
        middle, factor_two, gain_values[1], matmul_nt(query_grad, w_cq)
    )
    middle_grad = late_grad + norm_grad
    branch_grad = middle_grad.astype(BF16)
    keep, send = weight_grads(
        [
            (normed_two, query_grad),
            (encoder_states, kv_grad),
            (mixed_two, late_branch),
            (mixed_one, branch_grad),
        ],
        count,
    )
    mixed_grad = matmul_nt(branch_grad, w_so).astype(BF16)
    encoder_grad = matmul_nt(kv_grad, w_ckv).astype(BF16)
    middle_transfer = scatter_rows(keep, send, count)
    middle_gots = next(middle_transfer)
    middle_gots, mixed_grad, encoder_grad = tie(middle_gots, mixed_grad, encoder_grad)
    middle_gots = middle_transfer.send(middle_gots)
    qkv_grad, sheared = self_backward(qkv, mixed_grad, log_one, bias, length)
    middle_gots, qkv_grad, sheared = tie(middle_gots, qkv_grad, sheared)
    middle_gots = middle_transfer.send(middle_gots)
    keep, send = weight_grads([(normed_one, qkv_grad)], count)
    middle_gots, keep, send, qkv_grad = tie(middle_gots, keep, send, qkv_grad)
    middle_gots = middle_transfer.send(middle_gots)
    last_transfer = scatter_rows(keep, send, count)
    last_gots = next(last_transfer)
    norm_grad, gain_one = norm_backward(
        inputs, factor_one, gain_values[0], matmul_nt(qkv_grad, w_qkv)
    )
    input_grad = (middle_grad + norm_grad).astype(BF16)
    middle_gots, last_gots, input_grad, gain_one, feed_owned = tie(
        middle_gots, last_gots, input_grad, gain_one, feed_owned
    )
    last_gots = last_transfer.send(last_gots)
    middle_owned = finish(middle_transfer, middle_gots)
    by_distance = sum(
        jnp.pad(sheared[:, row, row:], ((0, 0), (0, row))) for row in range(sheared.shape[1])
    )
    table_part = jnp.sum(onehot[:, None, :] * by_distance[None, :, :], axis=-1)
    gains_part = jnp.stack([gain_one, gain_two, gain_three[0]])
    small = jnp.concatenate([gains_part.reshape(-1), table_part.reshape(-1)]).reshape(-1, 128)
    small_transfer = sum_everywhere(small, count)
    small_gots = next(small_transfer)
    while last_gots is not None:
        if small_gots is not None:
            last_gots, small_gots = tie(last_gots, small_gots)
            small_gots, small = step(small_transfer, small_gots)
        last_gots, self_owned = step(last_transfer, last_gots)
    if small_gots is not None:
        small = finish(small_transfer, small_gots)
    small = small.reshape(-1)
    o_gu, o_down = cut(feed_owned.astype(F32), FEED_WIDTHS)

    o_cq, o_ckv, o_co, o_so = cut(middle_owned, MIDDLE_WIDTHS)
    g_sq, g_sk, g_sv = flat_blocks(deinterleave(self_owned, 3, WIDE))
    g_cq, g_ck, g_cv, g_co, g_so = flat_blocks([o_cq] + deinterleave(o_ckv, 2, WIDE) + [o_co, o_so])
    g_gate, g_up = flat_blocks(deinterleave(o_gu, 2, CHUNK))
    g_down = unpack_down(o_down[None], FF // count)[0].reshape(-1)

    gains_grad = small[: 3 * D].reshape(3, D)
    table_grad = small[3 * D :].reshape(BUCKETS, HEADS)
    return (
        result_rows,
        input_grad,
        encoder_grad,
        g_sq,
        g_sk,
        g_sv,
        g_so,
        g_cq,
        g_ck,
        g_cv,
        g_co,
        g_gate,
        g_up,
        g_down,
        gains_grad,
        table_grad,
    )


def solution(mesh):
    flat = P("fsdp")
    rows = P("fsdp", None)
    return jax.shard_map(
        partial(per_device, mesh.shape["fsdp"]),
        mesh=mesh,
        in_specs=(rows, rows) + (flat,) * 11 + (P(), P(), P(), rows),
        out_specs=(rows, rows, rows) + (flat,) * 11 + (P(), P()),
        check_vma=False,
    )
```
